32 devices in a mesh: groups: 2 (over x), seq: 16 (over z, y, core).
Axes of the slice: x: 2, y: 2, z: 4, core: 2. Of those that a mesh axis runs over, the one named last changes fastest.
Arguments:
- queries: bfloat16 [16384, 2048], P(('groups', 'seq')), parts along dimension 0, may hold values from -10 to 10
- keys: bfloat16 [16384, 2048], P(('groups', 'seq')), parts along dimension 0, may hold values from -10 to 10
- values: bfloat16 [16384, 2048], P(('groups', 'seq')), parts along dimension 0, may hold values from -6 to 6
- ssd_input: bfloat16 [16384, 2048], P(('groups', 'seq')), parts along dimension 0, may hold values from -6 to 6
- bmat: bfloat16 [16384, 128], P(('groups', 'seq')), parts along dimension 0, may hold values from -0.5 to 0.5
- cmat: bfloat16 [16384, 128], P(('groups', 'seq')), parts along dimension 0, may hold values from -6 to 6
- expo: int32 [16384, 32], P(('groups', 'seq')), parts along dimension 0, may hold values from 1 to 16384
- rate: float32 [32], replicated, may hold values from 1.2207031e-05 to 0.06
- skip: float32 [32], replicated, may hold values from 0.5 to 1.5
Outputs:
- attn_out: bfloat16 [16384, 2048], P(('groups', 'seq')), parts along dimension 0
- normed_recurrence_output: bfloat16 [16384, 2048], P(('groups', 'seq')), parts along dimension 0
The draws below stay inside these ranges and needn't reach their ends.
There are 2 independent parts, one for each index of `groups`. The reference program is written for one: setup_inputs(seed, part) draws one part's arguments, and reference() takes and returns one part's arrays. A program takes and returns all parts, laid end to end along the dimension named above; an argument that names none is the same for every part. Nothing has to cross between parts.
All inputs are finite; a program needn't handle non-finite values.
Results may differ from the reference program's by a relative error of at most 0.0049.
Values may be sent and summed in bfloat16 or wider, within the bound.
No kernel may reach another device: no remote copies, remote signals or barrier semaphores. Data moves between devices by JAX's collectives and lax.ppermute only.
A program may use at most 192 MiB of HBM per device.

```python
import math
import jax
import jax.numpy as jnp
from jax import lax

HA = 16
E = 128
W = 2048
HS = 32
P_SIZE = 64
N = 128
Q = 256
DOCUMENT_LENGTH = 8192


def draw_queries(key, part):
    drawn = jnp.clip(1.6 * jax.random.normal(jax.random.fold_in(key, 1), (DOCUMENT_LENGTH, HA * E), jnp.float32), -10.0, 10.0)
    return drawn.astype(jnp.bfloat16)


def draw_keys(key, part):
    drawn = jnp.clip(1.6 * jax.random.normal(jax.random.fold_in(key, 2), (DOCUMENT_LENGTH, HA * E), jnp.float32), -10.0, 10.0)
    return drawn.astype(jnp.bfloat16)


def draw_expo(key, part):
    random_base_key, spike_random_key = jax.random.split(jax.random.fold_in(key, 11))
    base_values_list = jax.random.randint(random_base_key, (DOCUMENT_LENGTH, HS), 1, 4)
    spike_positions = jax.random.randint(spike_random_key, (4,), 0, DOCUMENT_LENGTH)
    spike_row_list = jnp.any(jnp.arange(DOCUMENT_LENGTH)[:, None] == spike_positions[None, :], axis=1)
    return jnp.where(spike_row_list[:, None], 2 * DOCUMENT_LENGTH, base_values_list).astype(jnp.int32)


def draw_rate(key, part):
    slow_key, fast_key, pick_key = jax.random.split(jax.random.fold_in(key, 13), 3)
    slow_rate = jnp.exp(jax.random.uniform(slow_key, (HS,), jnp.float32, math.log(0.1), math.log(0.22))) / DOCUMENT_LENGTH
    fast_rate = jnp.exp(jax.random.uniform(fast_key, (HS,), jnp.float32, math.log(0.02), math.log(0.06)))
    fast_heads = jax.random.uniform(pick_key, (HS,)) < 0.5
    return jnp.where(fast_heads, fast_rate, slow_rate).astype(jnp.float32)


def block_levels(own_key, dims, pieces, low, top_value):
    factor_of = 1.0
    for position, blocks in pieces:
        steps = jax.random.uniform(jax.random.fold_in(jax.random.fold_in(own_key, 6), position), (blocks,), jnp.float32, low / len(pieces), top_value / len(pieces))
        factor_of = factor_of * jnp.repeat(jnp.exp(steps), dims[position] // blocks).reshape((-1,) + (1,) * (len(dims) - 1 - position))
    return factor_of


def centred(stream_key, shape, scale, limit, cuts=(), kind=jnp.bfloat16):
    entries = scale * jax.random.normal(stream_key, shape, jnp.float32)
    if cuts:
        entries = entries * block_levels(stream_key, shape, cuts, -0.22, 0.18)
    return jnp.clip(entries, -limit, limit).astype(kind)


def setup_inputs(seed: int = 0, part: int = 0) -> dict:
    arg_keys = jax.random.split(jax.random.key(seed), 10)
    part_keys = jax.random.split(jax.random.fold_in(arg_keys[9], part), 10)
    queries = draw_queries(jax.random.fold_in(jax.random.fold_in(arg_keys[9], part), 71), part)
    keys = draw_keys(jax.random.fold_in(jax.random.fold_in(arg_keys[9], part), 71), part)
    values = centred(part_keys[2], (DOCUMENT_LENGTH, HA * E), 1.0, 6.0, ((0, 16),))
    ssd_input = centred(part_keys[3], (DOCUMENT_LENGTH, HS * P_SIZE), 1.0, 6.0, ((0, 16),))
    bmat = centred(part_keys[4], (DOCUMENT_LENGTH, N), N ** -0.5, 0.5, ((0, 16),))
    cmat = centred(part_keys[5], (DOCUMENT_LENGTH, N), 1.0, 6.0, ((0, 16),))
    expo = draw_expo(jax.random.fold_in(jax.random.fold_in(arg_keys[9], part), 71), part)
    rate = draw_rate(jax.random.fold_in(arg_keys[9], 71), part)
    skip = jnp.clip(jax.random.uniform(arg_keys[8], (HS,), jnp.float32, 0.5, 1.5), 0.5, 1.5)
    return {"queries": queries, "keys": keys, "values": values, "ssd_input": ssd_input, "bmat": bmat, "cmat": cmat, "expo": expo, "rate": rate, "skip": skip}


def block_local(piece_x, piece_b, piece_c, piece_loga):
    cumulative = jnp.cumsum(piece_loga, axis=0).T
    block_len = cumulative.shape[1]
    lower_mask = jnp.arange(block_len)[:, None] >= jnp.arange(block_len)[None, :]
    log_gaps = cumulative[:, :, None] - cumulative[:, None, :]
    decay_grid = jnp.where(lower_mask[None], jnp.exp(jnp.where(lower_mask[None], log_gaps, 0.0)), 0.0)
    cross_term = jnp.dot(piece_c, piece_b.T, preferred_element_type=jnp.float32)
    inner_term = (cross_term[None] * decay_grid).astype(jnp.bfloat16)
    intra_term = jnp.einsum('hts,shp->thp', inner_term.astype(jnp.float32), piece_x.astype(jnp.float32))
    end_weights = jnp.exp(cumulative[:, -1:] - cumulative)
    weighted = (end_weights.T[:, :, None] * piece_b.astype(jnp.float32)[:, None, :]).astype(jnp.bfloat16)
    local_state = jnp.einsum('shp,shn->hpn', piece_x.astype(jnp.float32), weighted.astype(jnp.float32))
    end_decay = jnp.exp(cumulative[:, -1])
    return (intra_term, cumulative, end_decay, local_state)

def block_output(intra_term, cumulative, piece_x, piece_c, skip, carried):
    inter_term = jnp.einsum('tn,hpn->thp', piece_c.astype(jnp.float32), carried, precision=lax.Precision.HIGHEST)
    mixed = intra_term + inter_term * jnp.exp(cumulative.T)[:, :, None] + skip[None, :, None] * piece_x.astype(jnp.float32)
    inv_rms = lax.rsqrt(lax.optimization_barrier(jnp.mean(mixed * mixed, axis=2, keepdims=True)) + 1e-05)
    return (mixed * inv_rms).astype(jnp.bfloat16).reshape(mixed.shape[0], mixed.shape[1] * mixed.shape[2])

def recurrence_ref(ssd_input, bmat, cmat, expo, rate, skip):
    block_count = DOCUMENT_LENGTH // Q
    all_x = ssd_input.reshape(block_count, Q, HS, P_SIZE)
    all_loga = (-rate[None, :] * expo.astype(jnp.float32)).reshape(block_count, Q, HS)
    all_b = bmat.reshape(block_count, Q, N)
    all_c = cmat.reshape(block_count, Q, N)

    def advance(carried, slices):
        piece_x, piece_b, piece_c, piece_loga = slices
        intra_term, cumulative, end_decay, local_state = block_local(piece_x, piece_b, piece_c, piece_loga)
        result = block_output(intra_term, cumulative, piece_x, piece_c, skip, carried)
        return (end_decay[:, None, None] * carried + local_state, result)
    start_state = jnp.zeros((HS, P_SIZE, N), jnp.float32)
    closing_state, outputs = lax.scan(advance, start_state, (all_x, all_b, all_c, all_loga))
    return outputs.reshape(DOCUMENT_LENGTH, HS * P_SIZE)

def attention_ref(queries, keys, values):
    block_rows = math.gcd(DOCUMENT_LENGTH, 512)
    zero_rows = jnp.zeros((W, HA * E), keys.dtype)
    keys_pad = jnp.concatenate([zero_rows, keys], axis=0)
    values_pad = jnp.concatenate([zero_rows, values], axis=0)

    def one_block(block_index):
        block_start = (block_index * block_rows).astype(jnp.int32)
        query_blk = lax.dynamic_slice_in_dim(queries, block_start, block_rows, 0).reshape(block_rows, HA, E).astype(jnp.float32)
        key_blk = lax.dynamic_slice_in_dim(keys_pad, block_start, block_rows + W, 0).reshape(block_rows + W, HA, E).astype(jnp.float32)
        value_blk = lax.dynamic_slice_in_dim(values_pad, block_start, block_rows + W, 0).reshape(block_rows + W, HA, E).astype(jnp.float32)
        query_pos = block_start + jnp.arange(block_rows, dtype=jnp.int32)
        key_pos = block_start - W + jnp.arange(block_rows + W, dtype=jnp.int32)
        visible = (key_pos[None, :] <= query_pos[:, None]) & (key_pos[None, :] > query_pos[:, None] - W) & (key_pos[None, :] >= 0)
        scores = jnp.einsum('rhe,khe->hrk', query_blk, key_blk) / math.sqrt(E)
        scores = jnp.where(visible[None], scores, -1e+30)
        row_max = lax.optimization_barrier(jnp.max(scores, axis=2, keepdims=True))
        exp_scores = jnp.exp(scores - row_max)
        attn_probs = (exp_scores / lax.optimization_barrier(jnp.sum(exp_scores, axis=2, keepdims=True))).astype(jnp.bfloat16)
        block_out = jnp.einsum('hrk,khe->rhe', attn_probs.astype(jnp.float32), value_blk)
        return block_out.reshape(block_rows, HA * E).astype(jnp.bfloat16)
    outputs = lax.map(one_block, jnp.arange(DOCUMENT_LENGTH // block_rows, dtype=jnp.int32))
    return outputs.reshape(DOCUMENT_LENGTH, HA * E)

def reference(queries, keys, values, ssd_input, bmat, cmat, expo, rate, skip):
    attn_out = attention_ref(queries, keys, values)
    normed_recurrence_output = recurrence_ref(ssd_input, bmat, cmat, expo, rate, skip)
    return (attn_out, normed_recurrence_output)
```

```python
import functools
import math

import jax
import jax.numpy as jnp
from jax import lax
from jax.experimental import pallas as pl
from jax.experimental.pallas import tpu as pltpu
from jax.sharding import PartitionSpec as P

E = 128
W = 2048
Q = 256
EPS = 1e-05
NEG = -1e30
CHUNK_HEADS = 2
VMEM = 48 * 1024 * 1024


def contract(a, b, dims):
    return lax.dot_general(a, b, (dims, ((), ())), preferred_element_type=jnp.float32)


def split_bf16(v, terms):
    parts = []
    for _ in range(terms):
        part = v.astype(jnp.bfloat16)
        parts.append(part)
        v = v - part.astype(jnp.float32)
    return parts


def attention_kernel(ok_ref, q_ref, ok0, ov0, zk, zv, yk, yv, ak, av, bk, bv, *rest):
    o_ref = rest[-1]
    rows = q_ref.shape[0]
    half = rows // 2
    scale = math.log2(math.e) / math.sqrt(E)
    row = lax.broadcasted_iota(jnp.int32, (half, half), 0)
    col = lax.broadcasted_iota(jnp.int32, (half, half), 1)
    lo, hi, whole = slice(0, half), slice(half, rows), slice(0, rows)
    for r in range(2):
        q = q_ref[r * half : (r + 1) * half, :]
        if r == 0:
            pieces = [
                (zk, zv, lo, col > row, 0),
                (zk, zv, hi, None, 0),
                (ok0, ov0, lo, col <= row, None),
            ]
        else:
            pieces = [
                (zk, zv, hi, col > row, 0),
                (ok0, ov0, lo, None, None),
                (ok0, ov0, hi, col <= row, None),
            ]
        pieces += [
            (ak, av, whole, None, 1),
            (yk, yv, whole, None, 2),
            (bk, bv, whole, None, 3),
        ]
        scores = []
        top = None
        for k_ref, _, part, mask, flag in pieces:
            s = contract(q, k_ref[part, :], ((1,), (1,)))
            if mask is not None:
                s = jnp.where(mask, s, NEG)
            m = jnp.max(s, axis=1, keepdims=True)
            if flag is not None:
                m = jnp.where(ok_ref[flag] > 0, m, NEG)
            top = m if top is None else jnp.maximum(top, m)
            scores.append(s)
        shift = top * (-scale)
        total = jnp.zeros((half, 1), jnp.float32)
        acc = jnp.zeros((half, E), jnp.float32)
        for s, (_, v_ref, part, mask, flag) in zip(scores, pieces):
            offset = shift
            if flag is not None:
                offset = jnp.where(ok_ref[flag] > 0, shift, NEG)
            p = jnp.exp2(s * scale + offset)
            total += jnp.sum(p, axis=1, keepdims=True)
            acc += contract(p.astype(jnp.bfloat16), v_ref[part, :], ((1,), (0,)))
        o_ref[r * half : (r + 1) * half, :] = (acc / total).astype(o_ref.dtype)


def attention_chunk(chunk, heads, flags, queries, keys, values, z, y, a, b, result):
    rows, width = queries.shape
    first = chunk * heads
    own = pl.BlockSpec((rows, E), lambda h: (0, first + h))
    key = pl.BlockSpec((rows, E), lambda h: (0, h))
    value = pl.BlockSpec((rows, E), lambda h: (0, heads + h))
    args = [flags, queries, keys, values, z, z, y, y, a, a, b, b]
    specs = [pl.BlockSpec(memory_space=pltpu.SMEM), own, own, own] + [key, value] * 4
    aliases = {}
    if result is not None:
        aliases = {len(args): 0}
        args.append(result)
        specs.append(pl.BlockSpec(memory_space=pl.ANY))
    seen = rows + W
    return pl.pallas_call(
        attention_kernel,
        grid=(heads,),
        in_specs=specs,
        out_specs=own,
        out_shape=jax.ShapeDtypeStruct((rows, width), jnp.bfloat16),
        input_output_aliases=aliases,
        compiler_params=pltpu.CompilerParams(vmem_limit_bytes=VMEM),
        cost_estimate=pl.CostEstimate(
            flops=heads * rows * seen * E * 8,
            bytes_accessed=heads * (2 * seen + 2 * rows) * E * 2,
            transcendentals=heads * rows * seen,
        ),
        name="attention",
    )(*args)


def running_expo(expo_ref):
    size = expo_ref.shape[0]
    expo = expo_ref[...]
    high = (expo >> 8).astype(jnp.float32).astype(jnp.bfloat16)
    low = (expo & 255).astype(jnp.float32).astype(jnp.bfloat16)
    row = lax.broadcasted_iota(jnp.int32, (size, size), 0)
    col = lax.broadcasted_iota(jnp.int32, (size, size), 1)
    lower = jnp.where(row >= col, 1.0, 0.0).astype(jnp.bfloat16)
    upper = jnp.where(row <= col, 1.0, 0.0).astype(jnp.bfloat16)
    down = contract(lower, high, ((1,), (0,))) * 256.0 + contract(lower, low, ((1,), (0,)))
    across = contract(high, upper, ((0,), (0,))) * 256.0 + contract(low, upper, ((0,), (0,)))
    return down, across


def pair_lanes(left, right, rows, dim):
    lane = lax.broadcasted_iota(jnp.int32, (rows, 2 * dim), 1)
    return jnp.where(lane < dim, left, right)


def states_kernel(dim, expo_ref, rate_ref, x_ref, b_ref, local_ref, total_ref, decay_ref):
    heads = expo_ref.shape[1]
    state = b_ref.shape[1]
    first = pl.program_id(0) == 0

    @pl.when(first)
    def _():
        total_ref[...] = jnp.zeros_like(total_ref)
        decay_ref[...] = jnp.ones_like(decay_ref)

    down, _ = running_expo(expo_ref)
    rate = rate_ref[...]
    end = down[-1:, :]
    weights = jnp.exp(rate * (down - end))
    end_decay = jnp.exp(-rate * end)
    b = b_ref[...].astype(jnp.float32)
    for pair in range(heads // 2):
        columns = slice(pair * 2 * dim, (pair + 1) * 2 * dim)
        x = x_ref[:, columns]
        made = []
        for h in (2 * pair, 2 * pair + 1):
            weighted = (weights[:, h : h + 1] * b).astype(jnp.bfloat16)
            made.append(contract(weighted, x, ((0,), (0,))))
        new = pair_lanes(made[0], made[1], state, dim)
        decay = pair_lanes(
            end_decay[:, 2 * pair : 2 * pair + 1],
            end_decay[:, 2 * pair + 1 : 2 * pair + 2],
            1,
            dim,
        )
        before = total_ref[:, columns]
        local_ref[:, columns] = before
        total_ref[:, columns] = before * decay + new
        decay_ref[:, columns] = decay_ref[:, columns] * decay


def intra_kernel(
    dim, expo_ref, rate_ref, rates_ref, skip_ref, x_ref, b_ref, c_ref, local_ref, pre_ref, factor_ref, past
):
    heads = expo_ref.shape[1]
    size = expo_ref.shape[0]
    half = size // 2

    @pl.when(pl.program_id(0) == 0)
    def _():
        past[...] = jnp.zeros_like(past)

    down, across = running_expo(expo_ref)
    rate = rate_ref[...]
    within = jnp.exp(-rate * down)
    factor_ref[...] = jnp.exp(-rate * (down + past[...]))
    past[...] = past[...] + down[-1:, :]
    c = c_ref[...]
    cross = contract(c, b_ref[...], ((1,), (1,)))
    row = lax.broadcasted_iota(jnp.int32, (half, half), 0)
    col = lax.broadcasted_iota(jnp.int32, (half, half), 1)
    seen = row >= col
    for pair in range(heads // 2):
        columns = slice(pair * 2 * dim, (pair + 1) * 2 * dim)
        x = x_ref[:, columns]
        xf = x.astype(jnp.float32)
        upper, lower = [], []
        for h in (2 * pair, 2 * pair + 1):
            r = rates_ref[h]
            here, there = down[:, h : h + 1], across[h : h + 1, :]
            gap = jnp.where(seen, (there[:, :half] - here[:half]) * r, NEG)
            inner = (cross[:half, :half] * jnp.exp(gap)).astype(jnp.bfloat16)
            upper.append(contract(inner, x[:half], ((1,), (0,))))
            gap = (there[:, :half] - here[half:]) * r
            inner_left = (cross[half:, :half] * jnp.exp(gap)).astype(jnp.bfloat16)
            gap = jnp.where(seen, (there[:, half:] - here[half:]) * r, NEG)
            inner_right = (cross[half:, half:] * jnp.exp(gap)).astype(jnp.bfloat16)
            inner = jnp.concatenate([inner_left, inner_right], axis=1)
            lower.append(contract(inner, x, ((1,), (0,))))
        intra = jnp.concatenate(
            [
                pair_lanes(upper[0], upper[1], half, dim),
                pair_lanes(lower[0], lower[1], half, dim),
            ],
            axis=0,
        )
        high, low = split_bf16(local_ref[:, columns], 2)
        carried = contract(c, high, ((1,), (0,))) + contract(c, low, ((1,), (0,)))
        decay = pair_lanes(
            within[:, 2 * pair : 2 * pair + 1], within[:, 2 * pair + 1 : 2 * pair + 2], size, dim
        )
        skip = pair_lanes(skip_ref[2 * pair], skip_ref[2 * pair + 1], 1, dim)
        pre_ref[:, columns] = intra + carried * decay + skip * xf


def final_kernel(dim, pre_ref, factor_ref, c_ref, entering_ref, o_ref):
    heads = factor_ref.shape[1]
    size = pre_ref.shape[0]
    c = c_ref[...]
    row = lax.broadcasted_iota(jnp.int32, (2 * dim, 2 * dim), 0) // dim
    col = lax.broadcasted_iota(jnp.int32, (2 * dim, 2 * dim), 1) // dim
    same = jnp.where(row == col, 1.0, 0.0).astype(jnp.bfloat16)
    for pair in range(heads // 2):
        columns = slice(pair * 2 * dim, (pair + 1) * 2 * dim)
        high, low = split_bf16(entering_ref[:, columns], 2)
        carried = contract(c, high, ((1,), (0,))) + contract(c, low, ((1,), (0,)))
        decay = pair_lanes(
            factor_ref[:, 2 * pair : 2 * pair + 1],
            factor_ref[:, 2 * pair + 1 : 2 * pair + 2],
            size,
            dim,
        )
        mixed = pre_ref[:, columns] + carried * decay
        high, low = split_bf16(mixed * mixed, 2)
        power = contract(high, same, ((1,), (0,))) + contract(low, same, ((1,), (0,)))
        o_ref[:, columns] = (mixed * lax.rsqrt(power * (1.0 / dim) + EPS)).astype(o_ref.dtype)


def recurrence_states(expo, rate, ssd_input, bmat):
    length, heads = expo.shape
    width, state = ssd_input.shape[1], bmat.shape[1]
    blocks = length // Q
    by_block = lambda n: pl.BlockSpec((Q, n), lambda b: (b, 0))
    once = lambda r, n: pl.BlockSpec((r, n), lambda b: (0, 0))
    return pl.pallas_call(
        functools.partial(states_kernel, width // heads),
        grid=(blocks,),
        in_specs=[by_block(heads), once(1, heads), by_block(width), by_block(state)],
        out_specs=[pl.BlockSpec((state, width), lambda b: (b, 0)), once(state, width), once(8, width)],
        out_shape=[
            jax.ShapeDtypeStruct((blocks * state, width), jnp.float32),
            jax.ShapeDtypeStruct((state, width), jnp.float32),
            jax.ShapeDtypeStruct((8, width), jnp.float32),
        ],
        compiler_params=pltpu.CompilerParams(vmem_limit_bytes=VMEM),
        cost_estimate=pl.CostEstimate(
            flops=length * width * state * 8, bytes_accessed=8 << 20, transcendentals=length * heads
        ),
        name="states",
    )(expo, rate[None], ssd_input, bmat)


def recurrence_intra(expo, rate, skip, ssd_input, bmat, cmat, local):
    length, heads = expo.shape
    width, state = ssd_input.shape[1], bmat.shape[1]
    blocks = length // Q
    by_block = lambda n: pl.BlockSpec((Q, n), lambda b: (b, 0))
    once = lambda r, n: pl.BlockSpec((r, n), lambda b: (0, 0))
    scalars = pl.BlockSpec(memory_space=pltpu.SMEM)
    return pl.pallas_call(
        functools.partial(intra_kernel, width // heads),
        grid=(blocks,),
        in_specs=[
            by_block(heads),
            once(1, heads),
            scalars,
            scalars,
            by_block(width),
            by_block(state),
            by_block(state),
            pl.BlockSpec((state, width), lambda b: (b, 0)),
        ],
        out_specs=[by_block(width), by_block(heads)],
        out_shape=[
            jax.ShapeDtypeStruct((length, width), jnp.float32),
            jax.ShapeDtypeStruct((length, heads), jnp.float32),
        ],
        scratch_shapes=[pltpu.VMEM((1, heads), jnp.float32)],
        compiler_params=pltpu.CompilerParams(vmem_limit_bytes=VMEM),
        cost_estimate=pl.CostEstimate(
            flops=length * width * Q * 8, bytes_accessed=12 << 20, transcendentals=length * heads * Q
        ),
        name="intra",
    )(expo, rate[None], rate, skip, ssd_input, bmat, cmat, local)


def recurrence_final(pre, factor, cmat, entering):
    length, width = pre.shape
    heads, state = factor.shape[1], cmat.shape[1]
    by_block = lambda n: pl.BlockSpec((Q, n), lambda b: (b, 0))
    return pl.pallas_call(
        functools.partial(final_kernel, width // heads),
        grid=(length // Q,),
        in_specs=[
            by_block(width),
            by_block(heads),
            by_block(state),
            pl.BlockSpec((state, width), lambda b: (0, 0)),
        ],
        out_specs=by_block(width),
        out_shape=jax.ShapeDtypeStruct((length, width), jnp.bfloat16),
        compiler_params=pltpu.CompilerParams(vmem_limit_bytes=VMEM),
        cost_estimate=pl.CostEstimate(
            flops=length * width * state * 8, bytes_accessed=8 << 20, transcendentals=length * heads
        ),
        name="final",
    )(pre, factor, cmat, entering)


def on_device(queries, keys, values, ssd_input, bmat, cmat, expo, rate, skip):
    length, width = queries.shape
    devices = lax.axis_size("seq")
    here = lax.axis_index("seq")
    span = W // length
    assert span == 4 and devices % span == 0 and length % (2 * Q) == 0
    planes = devices // span
    core, column = here % 2, (here // 2) % 2
    forward = [(i, i + span) for i in range(devices - span)]
    across = [(i, i ^ 2) for i in range(devices)]
    partner = [(i, i ^ 1) for i in range(devices)]
    send = lambda array, route: lax.ppermute(array, "seq", route)

    heads = width // E
    per = math.gcd(heads, CHUNK_HEADS)
    chunks = heads // per

    def packed(chunk):
        part = slice(chunk * per * E, (chunk + 1) * per * E)
        return jnp.concatenate([keys[:, part], values[:, part]], axis=1)

    near = jnp.where(core == 0, 3, 1)
    distance = jnp.stack([jnp.int32(4), near, jnp.int32(2), 4 - near])
    flags = (here >= distance).astype(jnp.int32)

    own = [packed(i) for i in range(chunks)]
    by_z = [send(part, forward) for part in own]
    by_y = [send(jnp.where(column == 0, o, z), across) for o, z in zip(own, by_z)]
    by_a = [send(jnp.where(core == 0, o, z), partner) for o, z in zip(own, by_z)]
    by_b = [send(y, partner) for y in by_y]

    local, total, decay = recurrence_states(expo, rate, ssd_input, bmat)
    pre, factor = recurrence_intra(expo, rate, skip, ssd_input, bmat, cmat, local)
    state = total.shape[0]
    both = jnp.concatenate([total, decay], axis=0)
    other = send(both, partner)
    first = jnp.where(core == 0, both, other)
    second = jnp.where(core == 0, other, both)
    first_total, first_decay = first[:state], first[state : state + 1]
    second_total, second_decay = second[:state], second[state : state + 1]
    wide = total.shape[1] // 2
    mine = lambda array: lax.dynamic_slice_in_dim(array, core * wide, wide, 1)
    chip_total = mine(second_decay * first_total + second_total)
    chip_decay = mine(first_decay * second_decay)
    rows = jnp.concatenate(
        [chip_total.astype(jnp.bfloat16)] + split_bf16(chip_decay, 3) + [jnp.zeros((13, wide), jnp.bfloat16)],
        axis=0,
    )
    got = send(rows, across).astype(jnp.float32)
    got_total = got[:state]
    got_decay = got[state : state + 1] + got[state + 1 : state + 2] + got[state + 2 : state + 3]
    plane_decay = chip_decay * got_decay
    plane_total = jnp.where(
        column == 0, got_decay * chip_total + got_total, chip_decay * got_total + chip_total
    )
    entering = jnp.zeros((state, wide), jnp.float32)
    for plane in range(planes - 1):
        route = [(plane * span + j, (plane + 1) * span + j) for j in range(span)]
        leaving = (plane_decay * entering + plane_total).astype(jnp.bfloat16)
        entering = entering + send(leaving, route).astype(jnp.float32)
    entering = jnp.where(column == 0, entering, got_decay * entering + got_total)
    theirs = send(entering, partner)
    entering = jnp.concatenate(
        [jnp.where(core == 0, entering, theirs), jnp.where(core == 0, theirs, entering)], axis=1
    )
    entering = jnp.where(core == 0, entering, first_decay * entering + first_total)

    attn_out = None
    for i in range(chunks):
        attn_out = attention_chunk(
            i, per, flags, queries, keys, values, by_z[i], by_y[i], by_a[i], by_b[i], attn_out
        )
    normed_recurrence_output = recurrence_final(pre, factor, cmat, entering)
    return (attn_out, normed_recurrence_output)


def solution(mesh):
    placed = P(("groups", "seq"), None)
    return jax.shard_map(
        on_device,
        mesh=mesh,
        in_specs=(placed,) * 7 + (P(), P()),
        out_specs=(placed, placed),
        check_vma=False,
    )
```

```python
import functools
import math

import jax
import jax.numpy as jnp
from jax import lax
from jax.experimental import pallas as pl
from jax.experimental.pallas import tpu as pltpu
from jax.sharding import PartitionSpec as P

E = 128
W = 2048
Q = 256
EPS = 1e-05
NEG = -1e30
SCALE = math.log2(math.e) / math.sqrt(E)
PAIR = 2
LENT = (2, 4, 4)
RELAYED = (2, 2, 2)
MIB = 1024 * 1024
HBM = pl.BlockSpec(memory_space=pl.ANY)
ON_CHIP = pl.BlockSpec(memory_space=pltpu.VMEM)
SCALARS = pl.BlockSpec(memory_space=pltpu.SMEM)


def params(mib):
    return pltpu.CompilerParams(vmem_limit_bytes=mib * MIB)


def contract(a, b, dims=((1,), (0,))):
    return lax.dot_general(a, b, (dims, ((), ())), preferred_element_type=jnp.float32)


def split_bf16(v, terms):
    parts = []
    for _ in range(terms):
        part = v.astype(jnp.bfloat16)
        parts.append(part)
        v = v - part.astype(jnp.float32)
    return parts


def split_contract(a, b, terms=2):
    return sum(contract(part, b) for part in split_bf16(a, terms))


def scaled(q):
    high, low = split_bf16(q.astype(jnp.float32) * SCALE, 2)
    return jnp.concatenate([high, low], axis=1)


def score(q, k, mask):
    s = contract(q, jnp.concatenate([k, k], axis=1), ((1,), (1,)))
    return s if mask is None else jnp.where(mask, s, NEG)


def weigh(s, top, v):
    p = jnp.exp2(s - top).astype(jnp.bfloat16)
    return contract(p, jnp.concatenate([v, jnp.ones_like(v)], axis=1))


def alternate(steps):
    steps = list(steps)
    while steps:
        for step in list(steps):
            try:
                next(step)
            except StopIteration:
                steps.remove(step)


def in_stages(tiles, first, second):
    kept = [{} for _ in tiles]
    alternate([first(*tiles[0], kept[0])])
    for i, tile in enumerate(tiles):
        ahead = [first(*tiles[i + 1], kept[i + 1])] if i + 1 < len(tiles) else []
        alternate(ahead + [second(*tile, kept[i])])
        kept[i].clear()


def lent_kernel(heads, side, q_ref, n_ref, ok, ov, pk, pv, yk, yv, bk, bv, _, o_ref, l_ref, m_ref):
    rows = q_ref.shape[0]
    half = rows // 2
    before = pl.program_id(0) * PAIR
    row = lax.broadcasted_iota(jnp.int32, (half, half), 0)
    col = lax.broadcasted_iota(jnp.int32, (half, half), 1)
    lane = lax.broadcasted_iota(jnp.int32, (half, E), 1)
    by_core, by_column = side[0] > 0, side[1] > 0
    causal, later = col <= row, col > row
    lo, hi = slice(0, half), slice(half, rows)

    @pl.when(before == 0)
    def _():
        l_ref[...] = jnp.zeros_like(l_ref)
        m_ref[:, heads * E :] = jnp.zeros((rows, E), m_ref.dtype)

    def first(h, r, kept):
        rr = (lo, hi)[r]
        cols = slice(h * E, (h + 1) * E)
        mine, lent = scaled(q_ref[rr, cols]), scaled(n_ref[rr, cols])
        core_q = jnp.where(by_core, mine, lent)
        column_q = jnp.where(by_column, mine, lent)
        own = (ok, ov)
        if r == 0:
            todo = [("mine", mine, own, lo, causal), ("lent", lent, own, lo, later), ("lent", lent, own, hi, None)]
        else:
            todo = [("mine", mine, own, lo, None), ("mine", mine, own, hi, causal), ("lent", lent, own, hi, later)]
        for name, q, shard in (
            ("core", core_q, (pk, pv)),
            ("column", column_q, (yk, yv)),
            ("column", column_q, (bk, bv)),
        ):
            todo += [(name, q, shard, part, None) for part in (lo, hi)]
        kept["top"], kept["scores"] = {}, []
        for name, q, (k_ref, v_ref), part, mask in todo:
            s = score(q, k_ref[part, cols], mask)
            m = jnp.max(s, axis=1, keepdims=True)
            tops = kept["top"]
            tops[name] = jnp.maximum(tops[name], m) if name in tops else m
            kept["scores"].append((name, s, v_ref, part))
            yield

    def second(h, r, kept):
        rr = (lo, hi)[r]
        cols = slice(h * E, (h + 1) * E)
        top = kept["top"]
        mine = jnp.maximum(top["mine"], jnp.maximum(jnp.where(by_core, top["core"], NEG), jnp.where(by_column, top["column"], NEG)))
        lent = jnp.maximum(top["lent"], jnp.maximum(jnp.where(by_core, NEG, top["core"]), jnp.where(by_column, NEG, top["column"])))
        limit = {
            "mine": mine,
            "lent": lent,
            "core": jnp.where(by_core, mine, lent),
            "column": jnp.where(by_column, mine, lent),
        }
        acc = {}
        for name, s, v_ref, part in kept["scores"]:
            a = weigh(s, limit[name], v_ref[part, cols])
            acc[name] = acc[name] + a if name in acc else a
            yield
        acc_mine = acc["mine"] + jnp.where(by_core, acc["core"], 0.0) + jnp.where(by_column, acc["column"], 0.0)
        acc_lent = acc["lent"] + jnp.where(by_core, 0.0, acc["core"]) + jnp.where(by_column, 0.0, acc["column"])
        o_ref[rr, cols] = acc_mine[:, :E] / acc_mine[:, E:]
        head = before + h
        at = pl.ds(pl.multiple_of(head * E, E), E)
        m_ref[rr, at] = (acc_lent[:, :E] / acc_lent[:, E:]).astype(m_ref.dtype)
        l_ref[rr, :] = jnp.where(lane == head, mine + jnp.log2(acc_mine[:, E:]), l_ref[rr, :])
        tail = slice(heads * E, (heads + 1) * E)
        stat = m_ref[rr, tail]
        for t, part in enumerate(split_bf16(lent + jnp.log2(acc_lent[:, E:]), 3)):
            stat = jnp.where(lane == 3 * head + t, part, stat)
        m_ref[rr, tail] = stat
        yield

    in_stages([(h, r) for h in range(PAIR) for r in range(2)], first, second)


def lent_heads(start, heads, offset, side, queries, asked, keys, values, pk, pv, y, b, after):
    rows = queries.shape[0]
    wide = PAIR * E
    pairs = heads // PAIR
    whole = pl.BlockSpec((rows, wide), lambda i: (0, start // PAIR + i))
    asked_at = pl.BlockSpec((rows, wide), lambda i: (0, offset // PAIR + i))
    part = pl.BlockSpec((rows, wide), lambda i: (0, i))
    later = pl.BlockSpec((rows, wide), lambda i: (0, pairs + i))
    fixed = lambda n: pl.BlockSpec((rows, n), lambda i: (0, 0))
    return pl.pallas_call(
        functools.partial(lent_kernel, heads),
        grid=(pairs,),
        in_specs=[SCALARS, whole, asked_at] + [whole] * 4 + [part, later] * 2 + [HBM],
        out_specs=[part, fixed(E), fixed((heads + 1) * E)],
        out_shape=[
            jax.ShapeDtypeStruct((rows, heads * E), jnp.float32),
            jax.ShapeDtypeStruct((rows, E), jnp.float32),
            jax.ShapeDtypeStruct((rows, (heads + 1) * E), jnp.bfloat16),
        ],
        compiler_params=params(60),
        cost_estimate=attention_cost(heads, rows),
        name="lent",
    )(side, queries, asked, keys, values, pk, pv, y, y, b, b, after)


def attention_cost(heads, rows):
    return pl.CostEstimate(
        flops=rows, bytes_accessed=rows, transcendentals=0
    )


def relayed_kernel(ok_ref, q_ref, ok, ov, zk, zv, ak, av, yk, yv, bk, bv, *rest):
    o_ref = rest[-1]
    rows = q_ref.shape[0]
    half = rows // 2
    row = lax.broadcasted_iota(jnp.int32, (half, half), 0)
    col = lax.broadcasted_iota(jnp.int32, (half, half), 1)
    causal, later = col <= row, col > row
    lo, hi = slice(0, half), slice(half, rows)

    def first(h, r, kept):
        cols = slice(h * E, (h + 1) * E)
        q = scaled(q_ref[(lo, hi)[r], cols])
        own, far = (ok, ov), (zk, zv)
        if r == 0:
            todo = [(own, lo, causal, None), (far, lo, later, 0), (far, hi, None, 0)]
        else:
            todo = [(own, lo, None, None), (own, hi, causal, None), (far, hi, later, 0)]
        for shard, flag in (((ak, av), 1), ((yk, yv), 2), ((bk, bv), 3)):
            todo += [(shard, part, None, flag) for part in (lo, hi)]
        kept["top"], kept["scores"] = None, []
        for (k_ref, v_ref), part, mask, flag in todo:
            s = score(q, k_ref[part, cols], mask)
            m = jnp.max(s, axis=1, keepdims=True)
            if flag is not None:
                m = jnp.where(ok_ref[flag] > 0, m, NEG)
            kept["top"] = m if kept["top"] is None else jnp.maximum(kept["top"], m)
            kept["scores"].append((s, v_ref, part, flag))
            yield

    def second(h, r, kept):
        top = kept["top"]
        acc = None
        cols = slice(h * E, (h + 1) * E)
        for s, v_ref, part, flag in kept["scores"]:
            limit = top if flag is None else jnp.where(ok_ref[flag] > 0, top, -NEG)
            a = weigh(s, limit, v_ref[part, cols])
            acc = a if acc is None else acc + a
            yield
        o_ref[(lo, hi)[r], cols] = (acc[:, :E] / acc[:, E:]).astype(o_ref.dtype)
        yield

    in_stages([(h, r) for h in range(PAIR) for r in range(2)], first, second)


def relayed_heads(start, offset, total, flags, queries, keys, values, z, a, y, b, result):
    rows, width = queries.shape
    wide = PAIR * E
    at = lambda n: pl.BlockSpec((rows, wide), lambda i: (0, n))
    own = at(start // PAIR)
    far = [at(offset // PAIR), at((total + offset) // PAIR)]
    args = [flags, queries, keys, values, z, z, a, a, y, y, b, b, result]
    return pl.pallas_call(
        relayed_kernel,
        grid=(1,),
        in_specs=[SCALARS] + [own] * 3 + far * 2 + [at(0), at(1)] * 2 + [HBM],
        out_specs=own,
        out_shape=jax.ShapeDtypeStruct((rows, width), jnp.bfloat16),
        input_output_aliases={len(args) - 1: 0},
        compiler_params=params(60),
        cost_estimate=attention_cost(PAIR, rows),
        name="relayed",
    )(*args)


def turn_kernel(count, column, own_ref, z_ref, _, *outs):
    wide = PAIR * E
    for j, out in enumerate(outs):
        for part in range(2):
            source = slice((part * count + j) * wide, (part * count + j + 1) * wide)
            out[:, part * wide : (part + 1) * wide] = jnp.where(
                column[0] == 0, own_ref[:, source], z_ref[:, source]
            )


def turn(count, column, own, z, after):
    rows = own.shape[0]
    by_tile = lambda n: pl.BlockSpec((rows // 2, n), lambda i: (i, 0))
    return pl.pallas_call(
        functools.partial(turn_kernel, count),
        grid=(2,),
        in_specs=[SCALARS, by_tile(own.shape[1]), by_tile(own.shape[1]), HBM],
        out_specs=[by_tile(2 * PAIR * E)] * count,
        out_shape=[jax.ShapeDtypeStruct((rows, 2 * PAIR * E), own.dtype)] * count,
        compiler_params=params(60),
        cost_estimate=pl.CostEstimate(flops=100, bytes_accessed=100, transcendentals=0),
        name="turn",
    )(column, own, z, after)


def join_kernel(ok_ref, mine_ref, l_ref, got_ref, stat_ref, *rest):
    o_ref = rest[-1]
    before = pl.program_id(0) * PAIR
    row = lax.broadcasted_iota(jnp.int32, (E, E), 0)
    col = lax.broadcasted_iota(jnp.int32, (E, E), 1)
    gather = jnp.where((row >= 3 * col) & (row < 3 * col + 3), 1.0, 0.0).astype(jnp.bfloat16)
    here = l_ref[...]
    there = jnp.where(ok_ref[0] > 0, contract(stat_ref[...], gather), NEG)
    top = jnp.maximum(here, there)
    here, there = jnp.exp2(here - top), jnp.exp2(there - top)
    share = split_bf16(here / (here + there), 2)
    for h in range(PAIR):
        cols = slice(h * E, (h + 1) * E)
        pick = jnp.where(row == before + h, 1.0, 0.0).astype(jnp.bfloat16)
        weight = sum(contract(part, pick) for part in share)
        back = got_ref[:, cols].astype(jnp.float32)
        o_ref[:, cols] = (back + weight * (mine_ref[:, cols] - back)).astype(o_ref.dtype)


def join(start, heads, flags, mine, l, got, width, result):
    rows = mine.shape[0]
    wide = PAIR * E
    part = pl.BlockSpec((rows, wide), lambda i: (0, i))
    args = [flags, mine, l, got, got]
    specs = [SCALARS, part, pl.BlockSpec((rows, E), lambda i: (0, 0)), part]
    specs.append(pl.BlockSpec((rows, E), lambda i: (0, heads)))
    aliases = {}
    if result is not None:
        aliases = {len(args): 0}
        args.append(result)
        specs.append(HBM)
    return pl.pallas_call(
        join_kernel,
        grid=(heads // PAIR,),
        in_specs=specs,
        out_specs=pl.BlockSpec((rows, wide), lambda i: (0, start // PAIR + i)),
        out_shape=jax.ShapeDtypeStruct((rows, width), jnp.bfloat16),
        input_output_aliases=aliases,
        compiler_params=params(60),
        cost_estimate=pl.CostEstimate(flops=rows, bytes_accessed=rows, transcendentals=0),
        name="join",
    )(*args)


def running_expo(expo_ref):
    size = expo_ref.shape[0]
    expo = expo_ref[...]
    high = (expo >> 8).astype(jnp.float32).astype(jnp.bfloat16)
    low = (expo & 255).astype(jnp.float32).astype(jnp.bfloat16)
    row = lax.broadcasted_iota(jnp.int32, (size, size), 0)
    col = lax.broadcasted_iota(jnp.int32, (size, size), 1)
    lower = jnp.where(row >= col, 1.0, 0.0).astype(jnp.bfloat16)
    upper = jnp.where(row <= col, 1.0, 0.0).astype(jnp.bfloat16)
    down = contract(lower, high) * 256.0 + contract(lower, low)
    across = contract(high, upper, ((0,), (0,))) * 256.0 + contract(low, upper, ((0,), (0,)))
    return down, across


def spread_matrix(heads, width):
    dim = width // heads
    head = lax.broadcasted_iota(jnp.int32, (heads, width), 0)
    col = lax.broadcasted_iota(jnp.int32, (heads, width), 1)
    inside = (col >= head * dim) & (col < head * dim + dim)
    return jnp.where(inside, 1.0, 0.0).astype(jnp.bfloat16)


def states_kernel(expo_ref, rate_ref, x_ref, b_ref, *refs):
    local_ref, both_ref = refs[-2:]
    heads, width, state = expo_ref.shape[1], x_ref.shape[1], b_ref.shape[1]

    @pl.when(pl.program_id(0) == 0)
    def _():
        both_ref[:state, :] = jnp.zeros((state, width), jnp.float32)
        both_ref[state:, :] = jnp.ones((8, width), jnp.float32)

    down, _ = running_expo(expo_ref)
    rate = rate_ref[...]
    end = down[-1:, :]
    spread = spread_matrix(heads, width)
    weights = split_contract(jnp.exp(rate * (down - end)), spread)
    decay = split_contract(jnp.broadcast_to(jnp.exp(-rate * end), (8, heads)), spread, 3)
    weighted = x_ref[...].astype(jnp.float32) * weights
    new = sum(contract(b_ref[...], part, ((0,), (0,))) for part in split_bf16(weighted, 2))
    before = both_ref[:state, :]
    local_ref[...] = before
    both_ref[:state, :] = before * decay[:1, :] + new
    both_ref[state:, :] = both_ref[state:, :] * decay


def intra_kernel(expo_ref, rate_ref, rates_ref, skip_ref, x_ref, b_ref, c_ref, local_ref, _, pre_ref, factor_ref, past):
    size, heads = expo_ref.shape
    width = x_ref.shape[1]
    dim = width // heads
    half = size // 2

    @pl.when(pl.program_id(0) == 0)
    def _():
        past[...] = jnp.zeros_like(past)

    down, across = running_expo(expo_ref)
    rate = rate_ref[...]
    factor_ref[...] = jnp.exp(-rate * (down + past[...]))
    past[...] = past[...] + down[-1:, :]
    c = c_ref[...]
    spread = spread_matrix(heads, width)
    within = split_contract(jnp.exp(-rate * down), spread)
    carried = sum(contract(c, part) for part in split_bf16(local_ref[...], 2))
    skip = split_contract(jnp.broadcast_to(skip_ref[...], (8, heads)), spread, 3)[:1, :]
    pre_ref[...] = carried * within + skip * x_ref[...].astype(jnp.float32)
    cross = contract(c, b_ref[...], ((1,), (1,)))
    row = lax.broadcasted_iota(jnp.int32, (half, half), 0)
    col = lax.broadcasted_iota(jnp.int32, (half, half), 1)
    seen = row >= col
    left = lax.broadcasted_iota(jnp.int32, (half, 2 * dim), 1) < dim
    for pair in range(heads // 2):
        columns = slice(pair * 2 * dim, (pair + 1) * 2 * dim)
        x = x_ref[:, columns]
        upper, lower = [], []
        for h in (2 * pair, 2 * pair + 1):
            r = rates_ref[h]
            here, there = down[:, h : h + 1], across[h : h + 1, :]
            gap = jnp.where(seen, (there[:, :half] - here[:half]) * r, NEG)
            inner = (cross[:half, :half] * jnp.exp(gap)).astype(jnp.bfloat16)
            upper.append(contract(inner, x[:half]))
            gap = (there[:, :half] - here[half:]) * r
            inner_left = (cross[half:, :half] * jnp.exp(gap)).astype(jnp.bfloat16)
            gap = jnp.where(seen, (there[:, half:] - here[half:]) * r, NEG)
            inner_right = (cross[half:, half:] * jnp.exp(gap)).astype(jnp.bfloat16)
            lower.append(contract(jnp.concatenate([inner_left, inner_right], axis=1), x))
        pre_ref[:half, columns] += jnp.where(left, upper[0], upper[1])
        pre_ref[half:, columns] += jnp.where(left, lower[0], lower[1])


def chip_kernel(core, both_ref, other_ref, *refs):
    chip_ref, rows_ref = refs[-2:]
    rows, width = both_ref.shape
    state = rows - 8
    wide = width // 2
    leads = core[0] == 0
    mine = jnp.where(leads, both_ref[:, :wide], both_ref[:, wide:])
    other = jnp.where(leads, other_ref[:, :wide], other_ref[:, wide:])
    first, second = jnp.where(leads, mine, other), jnp.where(leads, other, mine)
    total = first[:state] * second[state : state + 1] + second[:state]
    decay = first[state:] * second[state:]
    chip_ref[:state, :] = total
    chip_ref[state:, :] = decay
    rows_ref[:state, :] = total.astype(jnp.bfloat16)
    row = lax.broadcasted_iota(jnp.int32, (16, wide), 0)
    tail = jnp.zeros((16, wide), jnp.bfloat16)
    for t, part in enumerate(split_bf16(decay[:1, :], 3)):
        tail = jnp.where(row == t, part, tail)
    rows_ref[state:, :] = tail


def plane_kernel(column, chip_ref, got_ref, *refs):
    plane_ref, leaving_ref = refs[-2:]
    state = leaving_ref.shape[0]
    got = got_ref[...].astype(jnp.float32)
    got_total = got[:state]
    got_decay = got[state : state + 1] + got[state + 1 : state + 2] + got[state + 2 : state + 3]
    chip_total, chip_decay = chip_ref[:state, :], chip_ref[state : state + 1, :]
    total = jnp.where(
        column[0] == 0, chip_total * got_decay + got_total, got_total * chip_decay + chip_total
    )
    plane_ref[:state, :] = total
    plane_ref[state:, :] = chip_ref[state:, :] * got_decay
    leaving_ref[...] = total.astype(jnp.bfloat16)


def hop_kernel(plane_ref, entering_ref, came_ref, after_ref, leaving_ref):
    state = leaving_ref.shape[0]
    entering = entering_ref[...] + came_ref[...].astype(jnp.float32)
    after_ref[...] = entering
    leaving = entering * plane_ref[state : state + 1, :] + plane_ref[:state, :]
    leaving_ref[...] = leaving.astype(jnp.bfloat16)


def arrive_kernel(column, got_ref, entering_ref, came_ref, out_ref):
    state = came_ref.shape[0]
    entering = entering_ref[...] + came_ref[...].astype(jnp.float32)
    got = got_ref[...].astype(jnp.float32)
    got_decay = got[state : state + 1] + got[state + 1 : state + 2] + got[state + 2 : state + 3]
    out_ref[...] = jnp.where(column[0] == 0, entering, entering * got_decay + got[:state])


def final_kernel(core, pre_ref, factor_ref, c_ref, mine_ref, theirs_ref, other_ref, o_ref):
    size, width = pre_ref.shape
    heads = factor_ref.shape[1]
    state = mine_ref.shape[0]
    dim = width // heads
    wide = 2 * dim
    half = width // 2
    leads = core[0] == 0
    c = c_ref[...]
    row = lax.broadcasted_iota(jnp.int32, (wide, wide), 0) // dim
    col = lax.broadcasted_iota(jnp.int32, (wide, wide), 1) // dim
    same = jnp.where(row == col, 1.0, 0.0).astype(jnp.bfloat16)
    left = lax.broadcasted_iota(jnp.int32, (size, wide), 1) < dim
    for pair in range(heads // 2):
        columns = slice(pair * wide, (pair + 1) * wide)
        inner = slice(pair * wide % half, pair * wide % half + wide)
        mine, theirs = mine_ref[:, inner], theirs_ref[:, inner]
        first_half = pair * wide < half
        entering = jnp.where(leads, mine, theirs) if first_half else jnp.where(leads, theirs, mine)
        after_first = entering * other_ref[state : state + 1, columns] + other_ref[:state, columns]
        entering = jnp.where(leads, entering, after_first)
        carried = sum(contract(c, part) for part in split_bf16(entering, 2))
        factor = jnp.where(
            left, factor_ref[:, 2 * pair : 2 * pair + 1], factor_ref[:, 2 * pair + 1 : 2 * pair + 2]
        )
        mixed = pre_ref[:, columns] + carried * factor
        power = contract((mixed * mixed).astype(jnp.bfloat16), same)
        o_ref[:, columns] = (mixed * lax.rsqrt(power * (1.0 / dim) + EPS)).astype(o_ref.dtype)


def small(kernel, name, shapes, scalars, *args, after=()):
    late = list(after)
    return pl.pallas_call(
        kernel,
        in_specs=[SCALARS] * len(scalars) + [ON_CHIP] * len(args) + [HBM] * len(late),
        out_specs=[ON_CHIP] * len(shapes),
        out_shape=[jax.ShapeDtypeStruct(shape, kind) for shape, kind in shapes],
        compiler_params=params(16),
        cost_estimate=pl.CostEstimate(flops=100, bytes_accessed=100, transcendentals=0),
        name=name,
    )(*scalars, *args, *late)


def by_block(n):
    return pl.BlockSpec((Q, n), lambda b: (b, 0))


def once(r, n):
    return pl.BlockSpec((r, n), lambda b: (0, 0))


def recurrence_states(expo, rate, ssd_input, bmat, after):
    length, heads = expo.shape
    width, state = ssd_input.shape[1], bmat.shape[1]
    blocks = length // Q
    return pl.pallas_call(
        states_kernel,
        grid=(blocks,),
        in_specs=[by_block(heads), once(1, heads), by_block(width), by_block(state)] + [HBM] * len(after),
        out_specs=[pl.BlockSpec((state, width), lambda b: (b, 0)), once(state + 8, width)],
        out_shape=[
            jax.ShapeDtypeStruct((blocks * state, width), jnp.float32),
            jax.ShapeDtypeStruct((state + 8, width), jnp.float32),
        ],
        compiler_params=params(60),
        cost_estimate=pl.CostEstimate(
            flops=length, bytes_accessed=length, transcendentals=0
        ),
        name="states",
    )(expo, rate[None], ssd_input, bmat, *after)


def recurrence_intra(expo, rate, skip, ssd_input, bmat, cmat, local, after):
    length, heads = expo.shape
    width, state = ssd_input.shape[1], bmat.shape[1]
    blocks = length // Q
    return pl.pallas_call(
        intra_kernel,
        grid=(blocks,),
        in_specs=[
            by_block(heads),
            once(1, heads),
            SCALARS,
            once(1, heads),
            by_block(width),
            by_block(state),
            by_block(state),
            pl.BlockSpec((state, width), lambda b: (b, 0)),
            HBM,
        ],
        out_specs=[by_block(width), by_block(heads)],
        out_shape=[
            jax.ShapeDtypeStruct((length, width), jnp.float32),
            jax.ShapeDtypeStruct((length, heads), jnp.float32),
        ],
        scratch_shapes=[pltpu.VMEM((1, heads), jnp.float32)],
        compiler_params=params(60),
        cost_estimate=pl.CostEstimate(
            flops=length, bytes_accessed=length, transcendentals=0
        ),
        name="intra",
    )(expo, rate[None], rate, skip[None], ssd_input, bmat, cmat, local, after)


def recurrence_final(core, pre, factor, cmat, mine, theirs, other):
    length, width = pre.shape
    heads, state = factor.shape[1], cmat.shape[1]
    return pl.pallas_call(
        final_kernel,
        grid=(length // Q,),
        in_specs=[
            SCALARS,
            by_block(width),
            by_block(heads),
            by_block(state),
            once(*mine.shape),
            once(*theirs.shape),
            once(*other.shape),
        ],
        out_specs=by_block(width),
        out_shape=jax.ShapeDtypeStruct((length, width), jnp.bfloat16),
        compiler_params=params(60),
        cost_estimate=pl.CostEstimate(
            flops=length, bytes_accessed=length, transcendentals=0
        ),
        name="final",
    )(core, pre, factor, cmat, mine, theirs, other)


def on_device(queries, keys, values, ssd_input, bmat, cmat, expo, rate, skip):
    length, width = queries.shape
    devices = lax.axis_size("seq")
    here = lax.axis_index("seq")
    span = W // length
    assert span == 4 and devices % span == 0 and length % (2 * Q) == 0
    assert width == E * (sum(LENT) + sum(RELAYED))
    planes = devices // span
    core, column = here % 2, (here // 2) % 2
    core_1, column_1 = core[None].astype(jnp.int32), column[None].astype(jnp.int32)
    forward = [(i, i + span) for i in range(devices - span)]
    backward = [(j, i) for i, j in forward]
    across = [(i, i ^ 2) for i in range(devices)]
    partner = [(i, i ^ 1) for i in range(devices)]
    send = lambda array, route: lax.ppermute(array, "seq", route)

    starts = [sum(LENT[:i]) for i in range(len(LENT))]
    lent_total, relayed_total = sum(LENT), sum(RELAYED)
    columns = lambda array, s, n: array[:, s * E : (s + n) * E]
    packed = lambda s, n: jnp.concatenate([columns(keys, s, n), columns(values, s, n)], axis=1)

    by_y = [send(packed(s, n), across) for s, n in zip(starts, LENT)]
    asked_first = send(columns(queries, 0, LENT[0]), backward)
    asked_later = send(columns(queries, LENT[0], lent_total - LENT[0]), backward)
    to_z = packed(lent_total, relayed_total)
    by_z = send(to_z, forward)
    partner_k, partner_v = send(keys, partner), send(values, partner)
    by_b = [send(y, partner) for y in by_y]

    side = jnp.stack([core, column]).astype(jnp.int32)
    near = jnp.where(core == 0, 3, 1)
    distance = jnp.stack([jnp.int32(4), near, jnp.int32(2), 4 - near])
    flags = (here >= distance).astype(jnp.int32)

    def lent(i, after):
        asked, offset = (asked_first, 0) if i == 0 else (asked_later, starts[i] - LENT[0])
        return lent_heads(
            starts[i], LENT[i], offset, side, queries, asked, keys, values, partner_k, partner_v, by_y[i], by_b[i], after
        )

    local, both = recurrence_states(expo, rate, ssd_input, bmat, [by_y[0], asked_first])
    other = send(both, partner)
    partial = [lent(0, local)]
    pre, factor = recurrence_intra(expo, rate, skip, ssd_input, bmat, cmat, local, partial[0][1])
    state = bmat.shape[1]
    wide = ssd_input.shape[1] // 2
    full, brief = jnp.float32, jnp.bfloat16
    chip, rows = small(
        chip_kernel, "chip", [((state + 8, wide), full), ((state + 16, wide), brief)], [core_1], both, other, after=[factor, by_y[1]]
    )
    got = send(rows, across)
    partial.append(lent(1, chip))
    plane, leaving = small(
        plane_kernel, "plane", [((state + 8, wide), full), ((state, wide), brief)], [column_1], chip, got, after=[partial[1][1], by_y[2]]
    )
    by_a = send(jnp.where(core == 0, to_z, by_z), partner)
    turned = turn(len(RELAYED), column_1, to_z, by_z, partial[1][1])
    last_y = [send(part, across) for part in turned]
    last_b = [send(part, partner) for part in last_y]
    entering = jnp.zeros((state, wide), jnp.float32)
    for s in range(planes - 1):
        came = send(leaving, [(s * span + j, (s + 1) * span + j) for j in range(span)])
        if s == 0:
            partial.append(lent(2, plane))
        if s < planes - 2:
            entering, leaving = small(
                hop_kernel, "hop", [((state, wide), full), ((state, wide), brief)], [], plane, entering, came
            )
    (entering,) = small(arrive_kernel, "arrive", [((state, wide), full)], [column_1], got, entering, came)
    theirs = send(entering, partner)
    normed_recurrence_output = recurrence_final(core_1, pre, factor, cmat, entering, theirs, other)

    back = [send(message, forward) for _, _, message in partial]
    attn_out = None
    for i, (s, n) in enumerate(zip(starts[:-1], LENT)):
        attn_out = join(s, n, flags, partial[i][0], partial[i][1], back[i], width, attn_out)
    for i in range(len(RELAYED)):
        if i == len(RELAYED) - 1:
            attn_out = join(starts[-1], LENT[-1], flags, partial[-1][0], partial[-1][1], back[-1], width, attn_out)
        offset = sum(RELAYED[:i])
        attn_out = relayed_heads(
            lent_total + offset, offset, relayed_total, flags, queries, keys, values, by_z, by_a, last_y[i], last_b[i], attn_out
        )
    return (attn_out, normed_recurrence_output)


def solution(mesh):
    placed = P(("groups", "seq"), None)
    return jax.shard_map(
        on_device,
        mesh=mesh,
        in_specs=(placed,) * 7 + (P(), P()),
        out_specs=(placed, placed),
        check_vma=False,
    )
```

```python
import functools
import math

import jax
import jax.numpy as jnp
from jax import lax
from jax.experimental import pallas as pl
from jax.experimental.pallas import tpu as pltpu
from jax.sharding import PartitionSpec as P

E = 128
W = 2048
Q = 256
EPS = 1e-05
NEG = -1e30
SCALE = math.log2(math.e) / math.sqrt(E)
PAIR = 2
LENT = (2, 4, 4)
RELAYED = (2, 2, 2)
MIB = 1024 * 1024
HBM = pl.BlockSpec(memory_space=pl.ANY)
ON_CHIP = pl.BlockSpec(memory_space=pltpu.VMEM)
SCALARS = pl.BlockSpec(memory_space=pltpu.SMEM)


def params(mib):
    return pltpu.CompilerParams(vmem_limit_bytes=mib * MIB)


def contract(a, b, dims=((1,), (0,))):
    return lax.dot_general(a, b, (dims, ((), ())), preferred_element_type=jnp.float32)


def split_bf16(v, terms):
    parts = []
    for _ in range(terms):
        part = v.astype(jnp.bfloat16)
        parts.append(part)
        v = v - part.astype(jnp.float32)
    return parts


def split_contract(a, b, terms=2):
    return sum(contract(part, b) for part in split_bf16(a, terms))


def gate_kernel(array_ref, *refs):
    pass


def gate(array, *after):
    return pl.pallas_call(
        gate_kernel,
        in_specs=[HBM] * (1 + len(after)),
        out_specs=HBM,
        out_shape=jax.ShapeDtypeStruct(array.shape, array.dtype),
        input_output_aliases={0: 0},
        cost_estimate=pl.CostEstimate(flops=1, bytes_accessed=1, transcendentals=0),
        name="gate",
    )(array, *after)


def scaled(q):
    high, low = split_bf16(q.astype(jnp.float32) * SCALE, 2)
    return jnp.concatenate([high, low], axis=1)


def score(q, k, mask):
    s = contract(q, jnp.concatenate([k, k], axis=1), ((1,), (1,)))
    return s if mask is None else jnp.where(mask, s, NEG)


def weigh(s, top, v):
    p = jnp.exp2(s - top).astype(jnp.bfloat16)
    return contract(p, jnp.concatenate([v, jnp.ones_like(v)], axis=1))


def alternate(steps):
    steps = list(steps)
    while steps:
        for step in list(steps):
            try:
                next(step)
            except StopIteration:
                steps.remove(step)


def in_stages(tiles, first, second):
    kept = [{} for _ in tiles]
    alternate([first(*tiles[0], kept[0])])
    for i, tile in enumerate(tiles):
        ahead = [first(*tiles[i + 1], kept[i + 1])] if i + 1 < len(tiles) else []
        alternate(ahead + [second(*tile, kept[i])])
        kept[i].clear()


def lent_kernel(heads, side, q_ref, n_ref, ok, ov, pk, pv, yk, yv, bk, bv, _, o_ref, l_ref, m_ref):
    rows = q_ref.shape[0]
    half = rows // 2
    before = pl.program_id(0) * PAIR
    row = lax.broadcasted_iota(jnp.int32, (half, half), 0)
    col = lax.broadcasted_iota(jnp.int32, (half, half), 1)
    lane = lax.broadcasted_iota(jnp.int32, (half, E), 1)
    by_core, by_column = side[0] > 0, side[1] > 0
    causal, later = col <= row, col > row
    lo, hi = slice(0, half), slice(half, rows)

    @pl.when(before == 0)
    def _():
        l_ref[...] = jnp.zeros_like(l_ref)
        m_ref[:, heads * E :] = jnp.zeros((rows, E), m_ref.dtype)

    def first(h, r, kept):
        rr = (lo, hi)[r]
        cols = slice(h * E, (h + 1) * E)
        mine, lent = scaled(q_ref[rr, cols]), scaled(n_ref[rr, cols])
        core_q = jnp.where(by_core, mine, lent)
        column_q = jnp.where(by_column, mine, lent)
        own = (ok, ov)
        if r == 0:
            todo = [("mine", mine, own, lo, causal), ("lent", lent, own, lo, later), ("lent", lent, own, hi, None)]
        else:
            todo = [("mine", mine, own, lo, None), ("mine", mine, own, hi, causal), ("lent", lent, own, hi, later)]
        for name, q, shard in (
            ("core", core_q, (pk, pv)),
            ("column", column_q, (yk, yv)),
            ("column", column_q, (bk, bv)),
        ):
            todo += [(name, q, shard, part, None) for part in (lo, hi)]
        kept["top"], kept["scores"] = {}, []
        for name, q, (k_ref, v_ref), part, mask in todo:
            s = score(q, k_ref[part, cols], mask)
            m = jnp.max(s, axis=1, keepdims=True)
            tops = kept["top"]
            tops[name] = jnp.maximum(tops[name], m) if name in tops else m
            kept["scores"].append((name, s, v_ref, part))
            yield

    def second(h, r, kept):
        rr = (lo, hi)[r]
        cols = slice(h * E, (h + 1) * E)
        top = kept["top"]
        mine = jnp.maximum(top["mine"], jnp.maximum(jnp.where(by_core, top["core"], NEG), jnp.where(by_column, top["column"], NEG)))
        lent = jnp.maximum(top["lent"], jnp.maximum(jnp.where(by_core, NEG, top["core"]), jnp.where(by_column, NEG, top["column"])))
        limit = {
            "mine": mine,
            "lent": lent,
            "core": jnp.where(by_core, mine, lent),
            "column": jnp.where(by_column, mine, lent),
        }
        acc = {}
        for name, s, v_ref, part in kept["scores"]:
            a = weigh(s, limit[name], v_ref[part, cols])
            acc[name] = acc[name] + a if name in acc else a
            yield
        acc_mine = acc["mine"] + jnp.where(by_core, acc["core"], 0.0) + jnp.where(by_column, acc["column"], 0.0)
        acc_lent = acc["lent"] + jnp.where(by_core, 0.0, acc["core"]) + jnp.where(by_column, 0.0, acc["column"])
        o_ref[rr, cols] = acc_mine[:, :E] / acc_mine[:, E:]
        head = before + h
        at = pl.ds(pl.multiple_of(head * E, E), E)
        m_ref[rr, at] = (acc_lent[:, :E] / acc_lent[:, E:]).astype(m_ref.dtype)
        l_ref[rr, :] = jnp.where(lane == head, mine + jnp.log2(acc_mine[:, E:]), l_ref[rr, :])
        tail = slice(heads * E, (heads + 1) * E)
        stat = m_ref[rr, tail]
        for t, part in enumerate(split_bf16(lent + jnp.log2(acc_lent[:, E:]), 3)):
            stat = jnp.where(lane == 3 * head + t, part, stat)
        m_ref[rr, tail] = stat
        yield

    in_stages([(h, r) for h in range(PAIR) for r in range(2)], first, second)


def lent_heads(start, heads, offset, side, queries, asked, keys, values, pk, pv, y, b, after):
    rows = queries.shape[0]
    wide = PAIR * E
    pairs = heads // PAIR
    whole = pl.BlockSpec((rows, wide), lambda i: (0, start // PAIR + i))
    asked_at = pl.BlockSpec((rows, wide), lambda i: (0, offset // PAIR + i))
    part = pl.BlockSpec((rows, wide), lambda i: (0, i))
    later = pl.BlockSpec((rows, wide), lambda i: (0, pairs + i))
    fixed = lambda n: pl.BlockSpec((rows, n), lambda i: (0, 0))
    return pl.pallas_call(
        functools.partial(lent_kernel, heads),
        grid=(pairs,),
        in_specs=[SCALARS, whole, asked_at] + [whole] * 4 + [part, later] * 2 + [HBM],
        out_specs=[part, fixed(E), fixed((heads + 1) * E)],
        out_shape=[
            jax.ShapeDtypeStruct((rows, heads * E), jnp.float32),
            jax.ShapeDtypeStruct((rows, E), jnp.float32),
            jax.ShapeDtypeStruct((rows, (heads + 1) * E), jnp.bfloat16),
        ],
        compiler_params=params(60),
        cost_estimate=attention_cost(heads, rows),
        name="lent",
    )(side, queries, asked, keys, values, pk, pv, y, y, b, b, after)


def attention_cost(heads, rows):
    return pl.CostEstimate(flops=int(heads * rows * 1), bytes_accessed=rows, transcendentals=0)


def relayed_kernel(ok_ref, q_ref, ok, ov, zk, zv, ak, av, yk, yv, bk, bv, *rest):
    o_ref = rest[-1]
    rows = q_ref.shape[0]
    half = rows // 2
    row = lax.broadcasted_iota(jnp.int32, (half, half), 0)
    col = lax.broadcasted_iota(jnp.int32, (half, half), 1)
    causal, later = col <= row, col > row
    lo, hi = slice(0, half), slice(half, rows)

    def first(h, r, kept):
        cols = slice(h * E, (h + 1) * E)
        q = scaled(q_ref[(lo, hi)[r], cols])
        own, far = (ok, ov), (zk, zv)
        if r == 0:
            todo = [(own, lo, causal, None), (far, lo, later, 0), (far, hi, None, 0)]
        else:
            todo = [(own, lo, None, None), (own, hi, causal, None), (far, hi, later, 0)]
        for shard, flag in (((ak, av), 1), ((yk, yv), 2), ((bk, bv), 3)):
            todo += [(shard, part, None, flag) for part in (lo, hi)]
        kept["top"], kept["scores"] = None, []
        for (k_ref, v_ref), part, mask, flag in todo:
            s = score(q, k_ref[part, cols], mask)
            m = jnp.max(s, axis=1, keepdims=True)
            if flag is not None:
                m = jnp.where(ok_ref[flag] > 0, m, NEG)
            kept["top"] = m if kept["top"] is None else jnp.maximum(kept["top"], m)
            kept["scores"].append((s, v_ref, part, flag))
            yield

    def second(h, r, kept):
        top = kept["top"]
        acc = None
        cols = slice(h * E, (h + 1) * E)
        for s, v_ref, part, flag in kept["scores"]:
            limit = top if flag is None else jnp.where(ok_ref[flag] > 0, top, -NEG)
            a = weigh(s, limit, v_ref[part, cols])
            acc = a if acc is None else acc + a
            yield
        o_ref[(lo, hi)[r], cols] = (acc[:, :E] / acc[:, E:]).astype(o_ref.dtype)
        yield

    in_stages([(h, r) for h in range(PAIR) for r in range(2)], first, second)


def relayed_heads(start, offset, total, flags, queries, keys, values, z, a, y, b, result):
    rows, width = queries.shape
    wide = PAIR * E
    at = lambda n: pl.BlockSpec((rows, wide), lambda i: (0, n))
    own = at(start // PAIR)
    far = [at(offset // PAIR), at((total + offset) // PAIR)]
    args = [flags, queries, keys, values, z, z, a, a, y, y, b, b, result]
    return pl.pallas_call(
        relayed_kernel,
        grid=(1,),
        in_specs=[SCALARS] + [own] * 3 + far * 2 + [at(0), at(1)] * 2 + [HBM],
        out_specs=own,
        out_shape=jax.ShapeDtypeStruct((rows, width), jnp.bfloat16),
        input_output_aliases={len(args) - 1: 0},
        compiler_params=params(60),
        cost_estimate=attention_cost(PAIR, rows),
        name="relayed",
    )(*args)


def turn_kernel(count, column, own_ref, z_ref, _, *outs):
    wide = PAIR * E
    for j, out in enumerate(outs):
        for part in range(2):
            source = slice((part * count + j) * wide, (part * count + j + 1) * wide)
            out[:, part * wide : (part + 1) * wide] = jnp.where(
                column[0] == 0, own_ref[:, source], z_ref[:, source]
            )


def turn(count, column, own, z, after):
    rows = own.shape[0]
    by_tile = lambda n: pl.BlockSpec((rows // 2, n), lambda i: (i, 0))
    return pl.pallas_call(
        functools.partial(turn_kernel, count),
        grid=(2,),
        in_specs=[SCALARS, by_tile(own.shape[1]), by_tile(own.shape[1]), HBM],
        out_specs=[by_tile(2 * PAIR * E)] * count,
        out_shape=[jax.ShapeDtypeStruct((rows, 2 * PAIR * E), own.dtype)] * count,
        compiler_params=params(60),
        cost_estimate=pl.CostEstimate(flops=100, bytes_accessed=100, transcendentals=0),
        name="turn",
    )(column, own, z, after)


def join_kernel(ok_ref, mine_ref, l_ref, got_ref, stat_ref, *rest):
    o_ref = rest[-1]
    before = pl.program_id(0) * PAIR
    row = lax.broadcasted_iota(jnp.int32, (E, E), 0)
    col = lax.broadcasted_iota(jnp.int32, (E, E), 1)
    gather = jnp.where((row >= 3 * col) & (row < 3 * col + 3), 1.0, 0.0).astype(jnp.bfloat16)
    here = l_ref[...]
    there = jnp.where(ok_ref[0] > 0, contract(stat_ref[...], gather), NEG)
    top = jnp.maximum(here, there)
    here, there = jnp.exp2(here - top), jnp.exp2(there - top)
    share = split_bf16(here / (here + there), 2)
    for h in range(PAIR):
        cols = slice(h * E, (h + 1) * E)
        pick = jnp.where(row == before + h, 1.0, 0.0).astype(jnp.bfloat16)
        weight = sum(contract(part, pick) for part in share)
        back = got_ref[:, cols].astype(jnp.float32)
        o_ref[:, cols] = (back + weight * (mine_ref[:, cols] - back)).astype(o_ref.dtype)


def join(start, heads, flags, mine, l, got, width, after, result):
    rows = mine.shape[0]
    wide = PAIR * E
    part = pl.BlockSpec((rows, wide), lambda i: (0, i))
    args = [flags, mine, l, got, got]
    specs = [SCALARS, part, pl.BlockSpec((rows, E), lambda i: (0, 0)), part]
    specs.append(pl.BlockSpec((rows, E), lambda i: (0, heads)))
    args.append(after)
    specs.append(HBM)
    aliases = {}
    if result is not None:
        aliases = {len(args): 0}
        args.append(result)
        specs.append(HBM)
    return pl.pallas_call(
        join_kernel,
        grid=(heads // PAIR,),
        in_specs=specs,
        out_specs=pl.BlockSpec((rows, wide), lambda i: (0, start // PAIR + i)),
        out_shape=jax.ShapeDtypeStruct((rows, width), jnp.bfloat16),
        input_output_aliases=aliases,
        compiler_params=params(60),
        cost_estimate=pl.CostEstimate(flops=rows, bytes_accessed=rows, transcendentals=0),
        name="join",
    )(*args)


def running_expo(expo_ref):
    size = expo_ref.shape[1]
    expo = expo_ref[...]
    high = (expo >> 8).astype(jnp.float32).astype(jnp.bfloat16)
    low = (expo & 255).astype(jnp.float32).astype(jnp.bfloat16)
    row = lax.broadcasted_iota(jnp.int32, (size, size), 0)
    col = lax.broadcasted_iota(jnp.int32, (size, size), 1)
    lower = jnp.where(row >= col, 1.0, 0.0).astype(jnp.bfloat16)
    upper = jnp.where(row <= col, 1.0, 0.0).astype(jnp.bfloat16)
    down = contract(lower, high, ((1,), (1,))) * 256.0 + contract(lower, low, ((1,), (1,)))
    across = contract(high, upper) * 256.0 + contract(low, upper)
    return down, across


def spread_matrix(heads, width):
    dim = width // heads
    head = lax.broadcasted_iota(jnp.int32, (heads, width), 0)
    col = lax.broadcasted_iota(jnp.int32, (heads, width), 1)
    inside = (col >= head * dim) & (col < head * dim + dim)
    return jnp.where(inside, 1.0, 0.0).astype(jnp.bfloat16)


def states_kernel(expo_ref, rate_ref, x_ref, b_ref, *refs):
    local_ref, both_ref = refs[-2:]
    heads, width, state = expo_ref.shape[0], x_ref.shape[1], b_ref.shape[1]

    @pl.when(pl.program_id(0) == 0)
    def _():
        both_ref[:state, :] = jnp.zeros((state, width), jnp.float32)
        both_ref[state:, :] = jnp.ones((8, width), jnp.float32)

    down, _ = running_expo(expo_ref)
    rate = rate_ref[...]
    end = down[-1:, :]
    spread = spread_matrix(heads, width)
    weights = split_contract(jnp.exp(rate * (down - end)), spread)
    decay = split_contract(jnp.broadcast_to(jnp.exp(-rate * end), (8, heads)), spread, 3)
    weighted = x_ref[...].astype(jnp.float32) * weights
    new = sum(contract(b_ref[...], part, ((0,), (0,))) for part in split_bf16(weighted, 2))
    before = both_ref[:state, :]

    @pl.when(pl.program_id(0) > 0)
    def _():
        local_ref[...] = before

    both_ref[:state, :] = before * decay[:1, :] + new
    both_ref[state:, :] = both_ref[state:, :] * decay


def intra_kernel(expo_ref, rate_ref, rates_ref, skip_ref, x_ref, b_ref, c_ref, local_ref, _, pre_ref, factor_ref, past):
    heads, size = expo_ref.shape
    width = x_ref.shape[1]
    dim = width // heads
    half = size // 2

    @pl.when(pl.program_id(0) == 0)
    def _():
        past[...] = jnp.zeros_like(past)

    down, across = running_expo(expo_ref)
    rate = rate_ref[...]
    factor_ref[...] = jnp.exp(-rate * (down + past[...]))
    past[...] = past[...] + down[-1:, :]
    c = c_ref[...]
    spread = spread_matrix(heads, width)
    skip = split_contract(jnp.broadcast_to(skip_ref[...], (8, heads)), spread, 3)[:1, :]
    pre_ref[...] = skip * x_ref[...].astype(jnp.float32)

    @pl.when(pl.program_id(0) > 0)
    def _():
        within = split_contract(jnp.exp(-rate * down), spread)
        carried = sum(contract(c, part) for part in split_bf16(local_ref[...], 2))
        pre_ref[...] += carried * within

    cross = contract(c, b_ref[...], ((1,), (1,)))
    row = lax.broadcasted_iota(jnp.int32, (half, half), 0)
    col = lax.broadcasted_iota(jnp.int32, (half, half), 1)
    seen = row >= col
    left = lax.broadcasted_iota(jnp.int32, (half, 2 * dim), 1) < dim
    for pair in range(heads // 2):
        columns = slice(pair * 2 * dim, (pair + 1) * 2 * dim)
        x = x_ref[:, columns]
        upper, lower = [], []
        for h in (2 * pair, 2 * pair + 1):
            r = rates_ref[h]
            here, there = down[:, h : h + 1], across[h : h + 1, :]
            gap = jnp.where(seen, (there[:, :half] - here[:half]) * r, NEG)
            inner = (cross[:half, :half] * jnp.exp(gap)).astype(jnp.bfloat16)
            upper.append(contract(inner, x[:half]))
            gap = (there[:, :half] - here[half:]) * r
            inner_left = (cross[half:, :half] * jnp.exp(gap)).astype(jnp.bfloat16)
            gap = jnp.where(seen, (there[:, half:] - here[half:]) * r, NEG)
            inner_right = (cross[half:, half:] * jnp.exp(gap)).astype(jnp.bfloat16)
            lower.append(contract(jnp.concatenate([inner_left, inner_right], axis=1), x))
        pre_ref[:half, columns] += jnp.where(left, upper[0], upper[1])
        pre_ref[half:, columns] += jnp.where(left, lower[0], lower[1])


def chip_kernel(core, both_ref, other_ref, *refs):
    chip_ref, rows_ref = refs[-2:]
    rows, width = both_ref.shape
    state = rows - 8
    wide = width // 2
    leads = core[0] == 0
    mine = jnp.where(leads, both_ref[:, :wide], both_ref[:, wide:])
    other = jnp.where(leads, other_ref[:, :wide], other_ref[:, wide:])
    first, second = jnp.where(leads, mine, other), jnp.where(leads, other, mine)
    total = first[:state] * second[state : state + 1] + second[:state]
    decay = first[state:] * second[state:]
    chip_ref[:state, :] = total
    chip_ref[state:, :] = decay
    rows_ref[:state, :] = total.astype(jnp.bfloat16)
    row = lax.broadcasted_iota(jnp.int32, (16, wide), 0)
    tail = jnp.zeros((16, wide), jnp.bfloat16)
    for t, part in enumerate(split_bf16(decay[:1, :], 3)):
        tail = jnp.where(row == t, part, tail)
    rows_ref[state:, :] = tail


def plane_kernel(column, chip_ref, got_ref, *refs):
    plane_ref, leaving_ref = refs[-2:]
    state = leaving_ref.shape[0]
    got = got_ref[...].astype(jnp.float32)
    got_total = got[:state]
    got_decay = got[state : state + 1] + got[state + 1 : state + 2] + got[state + 2 : state + 3]
    chip_total, chip_decay = chip_ref[:state, :], chip_ref[state : state + 1, :]
    total = jnp.where(
        column[0] == 0, chip_total * got_decay + got_total, got_total * chip_decay + chip_total
    )
    plane_ref[:state, :] = total
    plane_ref[state:, :] = chip_ref[state:, :] * got_decay
    leaving_ref[...] = total.astype(jnp.bfloat16)


def hop_kernel(plane_ref, entering_ref, came_ref, after_ref, leaving_ref):
    state = leaving_ref.shape[0]
    entering = entering_ref[...] + came_ref[...].astype(jnp.float32)
    after_ref[...] = entering
    leaving = entering * plane_ref[state : state + 1, :] + plane_ref[:state, :]
    leaving_ref[...] = leaving.astype(jnp.bfloat16)


def arrive_kernel(column, got_ref, entering_ref, came_ref, out_ref):
    state = came_ref.shape[0]
    entering = entering_ref[...] + came_ref[...].astype(jnp.float32)
    got = got_ref[...].astype(jnp.float32)
    got_decay = got[state : state + 1] + got[state + 1 : state + 2] + got[state + 2 : state + 3]
    out_ref[...] = jnp.where(column[0] == 0, entering, entering * got_decay + got[:state])


def final_kernel(core, pre_ref, factor_ref, c_ref, mine_ref, theirs_ref, other_ref, o_ref):
    size, width = pre_ref.shape
    heads = factor_ref.shape[1]
    state = mine_ref.shape[0]
    dim = width // heads
    wide = 2 * dim
    half = width // 2
    leads = core[0] == 0
    c = c_ref[...]
    row = lax.broadcasted_iota(jnp.int32, (wide, wide), 0) // dim
    col = lax.broadcasted_iota(jnp.int32, (wide, wide), 1) // dim
    same = jnp.where(row == col, 1.0, 0.0).astype(jnp.bfloat16)
    left = lax.broadcasted_iota(jnp.int32, (size, wide), 1) < dim
    for pair in range(heads // 2):
        columns = slice(pair * wide, (pair + 1) * wide)
        inner = slice(pair * wide % half, pair * wide % half + wide)
        mine, theirs = mine_ref[:, inner], theirs_ref[:, inner]
        first_half = pair * wide < half
        entering = jnp.where(leads, mine, theirs) if first_half else jnp.where(leads, theirs, mine)
        after_first = entering * other_ref[state : state + 1, columns] + other_ref[:state, columns]
        entering = jnp.where(leads, entering, after_first)
        carried = sum(contract(c, part) for part in split_bf16(entering, 2))
        factor = jnp.where(
            left, factor_ref[:, 2 * pair : 2 * pair + 1], factor_ref[:, 2 * pair + 1 : 2 * pair + 2]
        )
        mixed = pre_ref[:, columns] + carried * factor
        power = contract((mixed * mixed).astype(jnp.bfloat16), same)
        o_ref[:, columns] = (mixed * lax.rsqrt(power * (1.0 / dim) + EPS)).astype(o_ref.dtype)


def small(kernel, name, shapes, scalars, *args, after=()):
    late = list(after)
    return pl.pallas_call(
        kernel,
        in_specs=[SCALARS] * len(scalars) + [ON_CHIP] * len(args) + [HBM] * len(late),
        out_specs=[ON_CHIP] * len(shapes),
        out_shape=[jax.ShapeDtypeStruct(shape, kind) for shape, kind in shapes],
        compiler_params=params(16),
        cost_estimate=pl.CostEstimate(flops=100, bytes_accessed=100, transcendentals=0),
        name=name,
    )(*scalars, *args, *late)


def by_block(n):
    return pl.BlockSpec((Q, n), lambda b: (b, 0))


def once(r, n):
    return pl.BlockSpec((r, n), lambda b: (0, 0))


def recurrence_states(expo, rate, ssd_input, bmat, after):
    heads, length = expo.shape
    width, state = ssd_input.shape[1], bmat.shape[1]
    blocks = length // Q
    return pl.pallas_call(
        states_kernel,
        grid=(blocks,),
        in_specs=[pl.BlockSpec((heads, Q), lambda b: (0, b)), once(1, heads), by_block(width), by_block(state)] + [HBM] * len(after),
        out_specs=[pl.BlockSpec((state, width), lambda b: (jnp.maximum(b - 1, 0), 0)), once(state + 8, width)],
        out_shape=[
            jax.ShapeDtypeStruct(((blocks - 1) * state, width), jnp.float32),
            jax.ShapeDtypeStruct((state + 8, width), jnp.float32),
        ],
        compiler_params=params(60),
        cost_estimate=pl.CostEstimate(
            flops=int(length * 1), bytes_accessed=length, transcendentals=0
        ),
        name="states",
    )(expo, rate[None], ssd_input, bmat, *after)


def recurrence_intra(expo, rate, skip, ssd_input, bmat, cmat, local, after):
    heads, length = expo.shape
    width, state = ssd_input.shape[1], bmat.shape[1]
    blocks = length // Q
    return pl.pallas_call(
        intra_kernel,
        grid=(blocks,),
        in_specs=[
            pl.BlockSpec((heads, Q), lambda b: (0, b)),
            once(1, heads),
            SCALARS,
            once(1, heads),
            by_block(width),
            by_block(state),
            by_block(state),
            pl.BlockSpec((state, width), lambda b: (jnp.maximum(b - 1, 0), 0)),
            HBM,
        ],
        out_specs=[by_block(width), by_block(heads)],
        out_shape=[
            jax.ShapeDtypeStruct((length, width), jnp.float32),
            jax.ShapeDtypeStruct((length, heads), jnp.float32),
        ],
        scratch_shapes=[pltpu.VMEM((1, heads), jnp.float32)],
        compiler_params=params(60),
        cost_estimate=pl.CostEstimate(
            flops=int(length * 1), bytes_accessed=length, transcendentals=0
        ),
        name="intra",
    )(expo, rate[None], rate, skip[None], ssd_input, bmat, cmat, local, after)


def recurrence_final(core, pre, factor, cmat, mine, theirs, other):
    length, width = pre.shape
    heads, state = factor.shape[1], cmat.shape[1]
    return pl.pallas_call(
        final_kernel,
        grid=(length // Q,),
        in_specs=[
            SCALARS,
            by_block(width),
            by_block(heads),
            by_block(state),
            once(*mine.shape),
            once(*theirs.shape),
            once(*other.shape),
        ],
        out_specs=by_block(width),
        out_shape=jax.ShapeDtypeStruct((length, width), jnp.bfloat16),
        compiler_params=params(24),
        cost_estimate=pl.CostEstimate(
            flops=int(length * 1), bytes_accessed=length, transcendentals=0
        ),
        name="final",
    )(core, pre, factor, cmat, mine, theirs, other)


def on_device(queries, keys, values, ssd_input, bmat, cmat, expo, rate, skip):
    length, width = queries.shape
    devices = lax.axis_size("seq")
    here = lax.axis_index("seq")
    span = W // length
    assert span == 4 and devices % span == 0 and length % (2 * Q) == 0
    assert width == E * (sum(LENT) + sum(RELAYED))
    planes = devices // span
    core, column = here % 2, (here // 2) % 2
    core_1, column_1 = core[None].astype(jnp.int32), column[None].astype(jnp.int32)
    forward = [(i, i + span) for i in range(devices - span)]
    backward = [(j, i) for i, j in forward]
    across = [(i, i ^ 2) for i in range(devices)]
    partner = [(i, i ^ 1) for i in range(devices)]
    send = lambda array, route: lax.ppermute(array, "seq", route)

    starts = [sum(LENT[:i]) for i in range(len(LENT))]
    lent_total, relayed_total = sum(LENT), sum(RELAYED)
    columns = lambda array, s, n: array[:, s * E : (s + n) * E]
    packed = lambda s, n: jnp.concatenate([columns(keys, s, n), columns(values, s, n)], axis=1)

    by_y = [send(packed(s, n), across) for s, n in zip(starts, LENT)]
    asked_first = send(columns(queries, 0, LENT[0]), backward)
    asked_later = send(columns(queries, LENT[0], lent_total - LENT[0]), backward)
    to_z = packed(lent_total, relayed_total)
    by_z = send(to_z, forward)
    partner_k, partner_v = send(keys, partner), send(values, partner)

    side = jnp.stack([core, column]).astype(jnp.int32)
    near = jnp.where(core == 0, 3, 1)
    distance = jnp.stack([jnp.int32(4), near, jnp.int32(2), 4 - near])
    flags = (here >= distance).astype(jnp.int32)

    def lent(i, after, y):
        asked, offset = (asked_first, 0) if i == 0 else (asked_later, starts[i] - LENT[0])
        return lent_heads(
            starts[i], LENT[i], offset, side, queries, asked, keys, values, partner_k, partner_v, y, send(y, partner), after
        )

    expo = expo.T
    local, both = recurrence_states(expo, rate, ssd_input, bmat, [])
    other = send(both, partner)
    partial = [lent(0, local, by_y[0])]
    pre, factor = recurrence_intra(expo, rate, skip, ssd_input, bmat, cmat, local, partial[0][1])
    state = bmat.shape[1]
    wide = ssd_input.shape[1] // 2
    full, brief = jnp.float32, jnp.bfloat16
    chip, rows = small(
        chip_kernel, "chip", [((state + 8, wide), full), ((state + 16, wide), brief)], [core_1], both, other, after=[factor, by_y[1]]
    )
    got = send(rows, across)
    partial.append(lent(1, chip, by_y[1]))
    plane, leaving = small(
        plane_kernel, "plane", [((state + 8, wide), full), ((state, wide), brief)], [column_1], chip, got, after=[partial[1][1]]
    )
    by_a = send(jnp.where(core == 0, to_z, by_z), partner)
    turned = turn(len(RELAYED), column_1, to_z, by_z, factor)
    last_y = [send(part, across) for part in turned]
    last_b = [send(part, partner) for part in last_y]
    entering = jnp.zeros((state, wide), jnp.float32)
    for s in range(planes - 1):
        came = send(leaving, [(s * span + j, (s + 1) * span + j) for j in range(span)])
        if s == 0:
            partial += [lent(i, plane, by_y[i]) for i in range(2, len(LENT))]
        if s < planes - 2:
            entering, leaving = small(
                hop_kernel, "hop", [((state, wide), full), ((state, wide), brief)], [], plane, entering, came
            )
    (entering,) = small(arrive_kernel, "arrive", [((state, wide), full)], [column_1], got, entering, came)
    theirs = send(entering, partner)
    normed_recurrence_output = recurrence_final(core_1, pre, factor, cmat, entering, theirs, other)

    back = [send(message, forward) for _, _, message in partial]
    attn_out = None
    for i, (s, n) in enumerate(zip(starts[:-1], LENT)):
        attn_out = join(s, n, flags, partial[i][0], partial[i][1], back[i], width, partial[-1][1], attn_out)
    for i in range(len(RELAYED)):
        if i == len(RELAYED) - 1:
            attn_out = join(starts[-1], LENT[-1], flags, partial[-1][0], partial[-1][1], back[-1], width, bmat, attn_out)
        offset = sum(RELAYED[:i])
        attn_out = relayed_heads(
            lent_total + offset, offset, relayed_total, flags, queries, keys, values, by_z, by_a, last_y[i], last_b[i], attn_out
        )
    return (attn_out, normed_recurrence_output)


def solution(mesh):
    placed = P(("groups", "seq"), None)
    return jax.shard_map(
        on_device,
        mesh=mesh,
        in_specs=(placed,) * 7 + (P(), P()),
        out_specs=(placed, placed),
        check_vma=False,
    )
```

```python
import functools
import math

import jax
import jax.numpy as jnp
from jax import lax
from jax.experimental import pallas as pl
from jax.experimental.pallas import tpu as pltpu
from jax.sharding import PartitionSpec as P

E = 128
W = 2048
Q = 256
EPS = 1e-05
NEG = -1e30
SCALE = math.log2(math.e) / math.sqrt(E)
PAIR = 2
LENT = (2, 4, 4)
RELAYED = (2, 2, 2)
MIB = 1024 * 1024
HBM = pl.BlockSpec(memory_space=pl.ANY)
ON_CHIP = pl.BlockSpec(memory_space=pltpu.VMEM)
SCALARS = pl.BlockSpec(memory_space=pltpu.SMEM)


def params(mib):
    return pltpu.CompilerParams(vmem_limit_bytes=mib * MIB)


def contract(a, b, dims=((1,), (0,))):
    return lax.dot_general(a, b, (dims, ((), ())), preferred_element_type=jnp.float32)


def split_bf16(v, terms):
    parts = []
    for _ in range(terms):
        part = v.astype(jnp.bfloat16)
        parts.append(part)
        v = v - part.astype(jnp.float32)
    return parts


def split_contract(a, b, terms=2):
    return sum(contract(part, b) for part in split_bf16(a, terms))


def gate_kernel(array_ref, *refs):
    pass


def gate(array, *after):
    return pl.pallas_call(
        gate_kernel,
        in_specs=[HBM] * (1 + len(after)),
        out_specs=HBM,
        out_shape=jax.ShapeDtypeStruct(array.shape, array.dtype),
        input_output_aliases={0: 0},
        cost_estimate=pl.CostEstimate(flops=1, bytes_accessed=1, transcendentals=0),
        name="gate",
    )(array, *after)


def scaled(q):
    high, low = split_bf16(q.astype(jnp.float32) * SCALE, 2)
    return jnp.concatenate([high, low], axis=1)


def score(q, k, mask):
    s = contract(q, jnp.concatenate([k, k], axis=1), ((1,), (1,)))
    return s if mask is None else jnp.where(mask, s, NEG)


def weigh(s, top, v):
    p = jnp.exp2(s - top).astype(jnp.bfloat16)
    return contract(p, jnp.concatenate([v, jnp.ones_like(v)], axis=1))


def alternate(steps):
    steps = list(steps)
    while steps:
        for step in list(steps):
            try:
                next(step)
            except StopIteration:
                steps.remove(step)


def in_stages(tiles, first, second):
    kept = [{} for _ in tiles]
    alternate([first(*tiles[0], kept[0])])
    for i, tile in enumerate(tiles):
        ahead = [first(*tiles[i + 1], kept[i + 1])] if i + 1 < len(tiles) else []
        alternate(ahead + [second(*tile, kept[i])])
        kept[i].clear()


def lent_kernel(heads, side, q_ref, n_ref, ok, ov, pk, pv, yk, yv, bk, bv, _, o_ref, l_ref, m_ref):
    rows = q_ref.shape[0]
    half = rows // 2
    before = pl.program_id(0) * PAIR
    row = lax.broadcasted_iota(jnp.int32, (half, half), 0)
    col = lax.broadcasted_iota(jnp.int32, (half, half), 1)
    lane = lax.broadcasted_iota(jnp.int32, (half, E), 1)
    by_core, by_column = side[0] > 0, side[1] > 0
    causal, later = col <= row, col > row
    lo, hi = slice(0, half), slice(half, rows)

    @pl.when(before == 0)
    def _():
        l_ref[...] = jnp.zeros_like(l_ref)
        m_ref[:, heads * E :] = jnp.zeros((rows, E), m_ref.dtype)

    def first(h, r, kept):
        rr = (lo, hi)[r]
        cols = slice(h * E, (h + 1) * E)
        mine, lent = scaled(q_ref[rr, cols]), scaled(n_ref[rr, cols])
        core_q = jnp.where(by_core, mine, lent)
        column_q = jnp.where(by_column, mine, lent)
        own = (ok, ov)
        if r == 0:
            todo = [("mine", mine, own, lo, causal), ("lent", lent, own, lo, later), ("lent", lent, own, hi, None)]
        else:
            todo = [("mine", mine, own, lo, None), ("mine", mine, own, hi, causal), ("lent", lent, own, hi, later)]
        for name, q, shard in (
            ("core", core_q, (pk, pv)),
            ("column", column_q, (yk, yv)),
            ("column", column_q, (bk, bv)),
        ):
            todo += [(name, q, shard, part, None) for part in (lo, hi)]
        kept["top"], kept["scores"] = {}, []
        for name, q, (k_ref, v_ref), part, mask in todo:
            s = score(q, k_ref[part, cols], mask)
            m = jnp.max(s, axis=1, keepdims=True)
            tops = kept["top"]
            tops[name] = jnp.maximum(tops[name], m) if name in tops else m
            kept["scores"].append((name, s, v_ref, part))
            yield

    def second(h, r, kept):
        rr = (lo, hi)[r]
        cols = slice(h * E, (h + 1) * E)
        top = kept["top"]
        mine = jnp.maximum(top["mine"], jnp.maximum(jnp.where(by_core, top["core"], NEG), jnp.where(by_column, top["column"], NEG)))
        lent = jnp.maximum(top["lent"], jnp.maximum(jnp.where(by_core, NEG, top["core"]), jnp.where(by_column, NEG, top["column"])))
        limit = {
            "mine": mine,
            "lent": lent,
            "core": jnp.where(by_core, mine, lent),
            "column": jnp.where(by_column, mine, lent),
        }
        acc = {}
        for name, s, v_ref, part in kept["scores"]:
            a = weigh(s, limit[name], v_ref[part, cols])
            acc[name] = acc[name] + a if name in acc else a
            yield
        acc_mine = acc["mine"] + jnp.where(by_core, acc["core"], 0.0) + jnp.where(by_column, acc["column"], 0.0)
        acc_lent = acc["lent"] + jnp.where(by_core, 0.0, acc["core"]) + jnp.where(by_column, 0.0, acc["column"])
        o_ref[rr, cols] = acc_mine[:, :E] / acc_mine[:, E:]
        head = before + h
        at = pl.ds(pl.multiple_of(head * E, E), E)
        m_ref[rr, at] = (acc_lent[:, :E] / acc_lent[:, E:]).astype(m_ref.dtype)
        l_ref[rr, :] = jnp.where(lane == head, mine + jnp.log2(acc_mine[:, E:]), l_ref[rr, :])
        tail = slice(heads * E, (heads + 1) * E)
        stat = m_ref[rr, tail]
        for t, part in enumerate(split_bf16(lent + jnp.log2(acc_lent[:, E:]), 3)):
            stat = jnp.where(lane == 3 * head + t, part, stat)
        m_ref[rr, tail] = stat
        yield

    in_stages([(h, r) for h in range(PAIR) for r in range(2)], first, second)


def lent_heads(start, heads, offset, side, queries, asked, keys, values, pk, pv, y, b, after):
    rows = queries.shape[0]
    wide = PAIR * E
    pairs = heads // PAIR
    whole = pl.BlockSpec((rows, wide), lambda i: (0, start // PAIR + i))
    asked_at = pl.BlockSpec((rows, wide), lambda i: (0, offset // PAIR + i))
    part = pl.BlockSpec((rows, wide), lambda i: (0, i))
    later = pl.BlockSpec((rows, wide), lambda i: (0, pairs + i))
    fixed = lambda n: pl.BlockSpec((rows, n), lambda i: (0, 0))
    return pl.pallas_call(
        functools.partial(lent_kernel, heads),
        grid=(pairs,),
        in_specs=[SCALARS, whole, asked_at] + [whole] * 4 + [part, later] * 2 + [HBM],
        out_specs=[part, fixed(E), fixed((heads + 1) * E)],
        out_shape=[
            jax.ShapeDtypeStruct((rows, heads * E), jnp.float32),
            jax.ShapeDtypeStruct((rows, E), jnp.float32),
            jax.ShapeDtypeStruct((rows, (heads + 1) * E), jnp.bfloat16),
        ],
        compiler_params=params(60),
        cost_estimate=attention_cost(heads, rows),
        name="lent",
    )(side, queries, asked, keys, values, pk, pv, y, y, b, b, after)


def attention_cost(heads, rows):
    return pl.CostEstimate(flops=int(heads * rows * 1), bytes_accessed=rows, transcendentals=0)


def relayed_kernel(ok_ref, q_ref, ok, ov, zk, zv, ak, av, yk, yv, bk, bv, *rest):
    o_ref = rest[-1]
    rows = q_ref.shape[0]
    half = rows // 2
    row = lax.broadcasted_iota(jnp.int32, (half, half), 0)
    col = lax.broadcasted_iota(jnp.int32, (half, half), 1)
    causal, later = col <= row, col > row
    lo, hi = slice(0, half), slice(half, rows)

    def first(h, r, kept):
        cols = slice(h * E, (h + 1) * E)
        q = scaled(q_ref[(lo, hi)[r], cols])
        own, far = (ok, ov), (zk, zv)
        if r == 0:
            todo = [(own, lo, causal, None), (far, lo, later, 0), (far, hi, None, 0)]
        else:
            todo = [(own, lo, None, None), (own, hi, causal, None), (far, hi, later, 0)]
        for shard, flag in (((ak, av), 1), ((yk, yv), 2), ((bk, bv), 3)):
            todo += [(shard, part, None, flag) for part in (lo, hi)]
        kept["top"], kept["scores"] = None, []
        for (k_ref, v_ref), part, mask, flag in todo:
            s = score(q, k_ref[part, cols], mask)
            m = jnp.max(s, axis=1, keepdims=True)
            if flag is not None:
                m = jnp.where(ok_ref[flag] > 0, m, NEG)
            kept["top"] = m if kept["top"] is None else jnp.maximum(kept["top"], m)
            kept["scores"].append((s, v_ref, part, flag))
            yield

    def second(h, r, kept):
        top = kept["top"]
        acc = None
        cols = slice(h * E, (h + 1) * E)
        for s, v_ref, part, flag in kept["scores"]:
            limit = top if flag is None else jnp.where(ok_ref[flag] > 0, top, -NEG)
            a = weigh(s, limit, v_ref[part, cols])
            acc = a if acc is None else acc + a
            yield
        o_ref[(lo, hi)[r], cols] = (acc[:, :E] / acc[:, E:]).astype(o_ref.dtype)
        yield

    in_stages([(h, r) for h in range(PAIR) for r in range(2)], first, second)


def relayed_heads(start, offset, total, flags, queries, keys, values, z, a, y, b, result):
    rows, width = queries.shape
    wide = PAIR * E
    at = lambda n: pl.BlockSpec((rows, wide), lambda i: (0, n))
    own = at(start // PAIR)
    far = [at(offset // PAIR), at((total + offset) // PAIR)]
    args = [flags, queries, keys, values, z, z, a, a, y, y, b, b, result]
    return pl.pallas_call(
        relayed_kernel,
        grid=(1,),
        in_specs=[SCALARS] + [own] * 3 + far * 2 + [at(0), at(1)] * 2 + [HBM],
        out_specs=own,
        out_shape=jax.ShapeDtypeStruct((rows, width), jnp.bfloat16),
        input_output_aliases={len(args) - 1: 0},
        compiler_params=params(60),
        cost_estimate=attention_cost(PAIR, rows),
        name="relayed",
    )(*args)


def turn_kernel(count, column, own_ref, z_ref, _, *outs):
    wide = PAIR * E
    for j, out in enumerate(outs):
        for part in range(2):
            source = slice((part * count + j) * wide, (part * count + j + 1) * wide)
            out[:, part * wide : (part + 1) * wide] = jnp.where(
                column[0] == 0, own_ref[:, source], z_ref[:, source]
            )


def turn(count, column, own, z, after):
    rows = own.shape[0]
    by_tile = lambda n: pl.BlockSpec((rows // 2, n), lambda i: (i, 0))
    return pl.pallas_call(
        functools.partial(turn_kernel, count),
        grid=(2,),
        in_specs=[SCALARS, by_tile(own.shape[1]), by_tile(own.shape[1]), HBM],
        out_specs=[by_tile(2 * PAIR * E)] * count,
        out_shape=[jax.ShapeDtypeStruct((rows, 2 * PAIR * E), own.dtype)] * count,
        compiler_params=params(60),
        cost_estimate=pl.CostEstimate(flops=100, bytes_accessed=100, transcendentals=0),
        name="turn",
    )(column, own, z, after)


def join_kernel(ok_ref, mine_ref, l_ref, got_ref, stat_ref, *rest):
    o_ref = rest[-1]
    before = pl.program_id(0) * PAIR
    row = lax.broadcasted_iota(jnp.int32, (E, E), 0)
    col = lax.broadcasted_iota(jnp.int32, (E, E), 1)
    gather = jnp.where((row >= 3 * col) & (row < 3 * col + 3), 1.0, 0.0).astype(jnp.bfloat16)
    here = l_ref[...]
    there = jnp.where(ok_ref[0] > 0, contract(stat_ref[...], gather), NEG)
    top = jnp.maximum(here, there)
    here, there = jnp.exp2(here - top), jnp.exp2(there - top)
    share = split_bf16(here / (here + there), 2)
    for h in range(PAIR):
        cols = slice(h * E, (h + 1) * E)
        pick = jnp.where(row == before + h, 1.0, 0.0).astype(jnp.bfloat16)
        weight = sum(contract(part, pick) for part in share)
        back = got_ref[:, cols].astype(jnp.float32)
        o_ref[:, cols] = (back + weight * (mine_ref[:, cols] - back)).astype(o_ref.dtype)


def join(start, heads, flags, mine, l, got, width, after, result):
    rows = mine.shape[0]
    wide = PAIR * E
    part = pl.BlockSpec((rows, wide), lambda i: (0, i))
    args = [flags, mine, l, got, got]
    specs = [SCALARS, part, pl.BlockSpec((rows, E), lambda i: (0, 0)), part]
    specs.append(pl.BlockSpec((rows, E), lambda i: (0, heads)))
    args.append(after)
    specs.append(HBM)
    aliases = {}
    if result is not None:
        aliases = {len(args): 0}
        args.append(result)
        specs.append(HBM)
    return pl.pallas_call(
        join_kernel,
        grid=(heads // PAIR,),
        in_specs=specs,
        out_specs=pl.BlockSpec((rows, wide), lambda i: (0, start // PAIR + i)),
        out_shape=jax.ShapeDtypeStruct((rows, width), jnp.bfloat16),
        input_output_aliases=aliases,
        compiler_params=params(60),
        cost_estimate=pl.CostEstimate(flops=rows, bytes_accessed=rows, transcendentals=0),
        name="join",
    )(*args)


def running_expo(expo_ref):
    size = expo_ref.shape[1]
    expo = expo_ref[...]
    high = (expo >> 8).astype(jnp.float32).astype(jnp.bfloat16)
    low = (expo & 255).astype(jnp.float32).astype(jnp.bfloat16)
    row = lax.broadcasted_iota(jnp.int32, (size, size), 0)
    col = lax.broadcasted_iota(jnp.int32, (size, size), 1)
    lower = jnp.where(row >= col, 1.0, 0.0).astype(jnp.bfloat16)
    upper = jnp.where(row <= col, 1.0, 0.0).astype(jnp.bfloat16)
    down = contract(lower, high, ((1,), (1,))) * 256.0 + contract(lower, low, ((1,), (1,)))
    across = contract(high, upper) * 256.0 + contract(low, upper)
    return down, across


def spread_matrix(heads, width):
    dim = width // heads
    head = lax.broadcasted_iota(jnp.int32, (heads, width), 0)
    col = lax.broadcasted_iota(jnp.int32, (heads, width), 1)
    inside = (col >= head * dim) & (col < head * dim + dim)
    return jnp.where(inside, 1.0, 0.0).astype(jnp.bfloat16)


def states_kernel(expo_ref, rate_ref, x_ref, b_ref, *refs):
    local_ref, both_ref = refs[-2:]
    heads, width, state = expo_ref.shape[0], x_ref.shape[1], b_ref.shape[1]

    @pl.when(pl.program_id(0) == 0)
    def _():
        both_ref[:state, :] = jnp.zeros((state, width), jnp.float32)
        both_ref[state:, :] = jnp.ones((8, width), jnp.float32)

    down, _ = running_expo(expo_ref)
    rate = rate_ref[...]
    end = down[-1:, :]
    spread = spread_matrix(heads, width)
    weights = split_contract(jnp.exp(rate * (down - end)), spread)
    decay = split_contract(jnp.broadcast_to(jnp.exp(-rate * end), (8, heads)), spread, 3)
    weighted = x_ref[...].astype(jnp.float32) * weights
    new = sum(contract(b_ref[...], part, ((0,), (0,))) for part in split_bf16(weighted, 2))
    before = both_ref[:state, :]

    @pl.when(pl.program_id(0) > 0)
    def _():
        local_ref[...] = before

    both_ref[:state, :] = before * decay[:1, :] + new
    both_ref[state:, :] = both_ref[state:, :] * decay


def intra_kernel(expo_ref, rate_ref, rates_ref, skip_ref, x_ref, b_ref, c_ref, local_ref, _, pre_ref, factor_ref, past):
    heads, size = expo_ref.shape
    width = x_ref.shape[1]
    dim = width // heads
    half = size // 2

    @pl.when(pl.program_id(0) == 0)
    def _():
        past[...] = jnp.zeros_like(past)

    down, across = running_expo(expo_ref)
    rate = rate_ref[...]
    factor_ref[...] = jnp.exp(-rate * (down + past[...]))
    past[...] = past[...] + down[-1:, :]
    c = c_ref[...]
    spread = spread_matrix(heads, width)
    skip = split_contract(jnp.broadcast_to(skip_ref[...], (8, heads)), spread, 3)[:1, :]
    pre_ref[...] = skip * x_ref[...].astype(jnp.float32)

    @pl.when(pl.program_id(0) > 0)
    def _():
        within = split_contract(jnp.exp(-rate * down), spread)
        carried = sum(contract(c, part) for part in split_bf16(local_ref[...], 2))
        pre_ref[...] += carried * within

    cross = contract(c, b_ref[...], ((1,), (1,)))
    row = lax.broadcasted_iota(jnp.int32, (half, half), 0)
    col = lax.broadcasted_iota(jnp.int32, (half, half), 1)
    seen = row >= col
    left = lax.broadcasted_iota(jnp.int32, (half, 2 * dim), 1) < dim
    for pair in range(heads // 2):
        columns = slice(pair * 2 * dim, (pair + 1) * 2 * dim)
        x = x_ref[:, columns]
        upper, lower = [], []
        for h in (2 * pair, 2 * pair + 1):
            r = rates_ref[h] * math.log2(math.e)
            here, there = down[:, h : h + 1], across[h : h + 1, :]
            gap = jnp.where(seen, (there[:, :half] - here[:half]) * r, NEG)
            inner = (cross[:half, :half] * jnp.exp2(gap)).astype(jnp.bfloat16)
            upper.append(contract(inner, x[:half]))
            gap = (there[:, :half] - here[half:]) * r
            inner_left = (cross[half:, :half] * jnp.exp2(gap)).astype(jnp.bfloat16)
            gap = jnp.where(seen, (there[:, half:] - here[half:]) * r, NEG)
            inner_right = (cross[half:, half:] * jnp.exp2(gap)).astype(jnp.bfloat16)
            lower.append(contract(jnp.concatenate([inner_left, inner_right], axis=1), x))
        pre_ref[:half, columns] += jnp.where(left, upper[0], upper[1])
        pre_ref[half:, columns] += jnp.where(left, lower[0], lower[1])


def chip_kernel(core, both_ref, other_ref, *refs):
    chip_ref, rows_ref = refs[-2:]
    rows, width = both_ref.shape
    state = rows - 8
    wide = width // 2
    leads = core[0] == 0
    mine = jnp.where(leads, both_ref[:, :wide], both_ref[:, wide:])
    other = jnp.where(leads, other_ref[:, :wide], other_ref[:, wide:])
    first, second = jnp.where(leads, mine, other), jnp.where(leads, other, mine)
    total = first[:state] * second[state : state + 1] + second[:state]
    decay = first[state:] * second[state:]
    chip_ref[:state, :] = total
    chip_ref[state:, :] = decay
    rows_ref[:state, :] = total.astype(jnp.bfloat16)
    row = lax.broadcasted_iota(jnp.int32, (16, wide), 0)
    tail = jnp.zeros((16, wide), jnp.bfloat16)
    for t, part in enumerate(split_bf16(decay[:1, :], 3)):
        tail = jnp.where(row == t, part, tail)
    rows_ref[state:, :] = tail


def plane_kernel(column, chip_ref, got_ref, *refs):
    plane_ref, leaving_ref = refs[-2:]
    state = leaving_ref.shape[0]
    got = got_ref[...].astype(jnp.float32)
    got_total = got[:state]
    got_decay = got[state : state + 1] + got[state + 1 : state + 2] + got[state + 2 : state + 3]
    chip_total, chip_decay = chip_ref[:state, :], chip_ref[state : state + 1, :]
    total = jnp.where(
        column[0] == 0, chip_total * got_decay + got_total, got_total * chip_decay + chip_total
    )
    plane_ref[:state, :] = total
    plane_ref[state:, :] = chip_ref[state:, :] * got_decay
    leaving_ref[...] = total.astype(jnp.bfloat16)


def hop_kernel(plane_ref, entering_ref, came_ref, after_ref, leaving_ref):
    state = leaving_ref.shape[0]
    entering = entering_ref[...] + came_ref[...].astype(jnp.float32)
    after_ref[...] = entering
    leaving = entering * plane_ref[state : state + 1, :] + plane_ref[:state, :]
    leaving_ref[...] = leaving.astype(jnp.bfloat16)


def arrive_kernel(column, got_ref, entering_ref, came_ref, out_ref):
    state = came_ref.shape[0]
    entering = entering_ref[...] + came_ref[...].astype(jnp.float32)
    got = got_ref[...].astype(jnp.float32)
    got_decay = got[state : state + 1] + got[state + 1 : state + 2] + got[state + 2 : state + 3]
    out_ref[...] = jnp.where(column[0] == 0, entering, entering * got_decay + got[:state])


def final_kernel(core, pre_ref, factor_ref, c_ref, mine_ref, theirs_ref, other_ref, o_ref, high_ref, low_ref):
    size, width = pre_ref.shape
    heads = factor_ref.shape[1]
    state = mine_ref.shape[0]
    dim = width // heads
    wide = 2 * dim
    half = width // 2
    leads = core[0] == 0

    @pl.when(pl.program_id(0) == 0)
    def _():
        mine, theirs = mine_ref[...], theirs_ref[...]
        for side, entering in enumerate((jnp.where(leads, mine, theirs), jnp.where(leads, theirs, mine))):
            columns = slice(side * half, (side + 1) * half)
            after_first = entering * other_ref[state : state + 1, columns] + other_ref[:state, columns]
            high, low = split_bf16(jnp.where(leads, entering, after_first), 2)
            high_ref[:, columns] = high
            low_ref[:, columns] = low

    c = c_ref[...]
    row = lax.broadcasted_iota(jnp.int32, (wide, wide), 0) // dim
    col = lax.broadcasted_iota(jnp.int32, (wide, wide), 1) // dim
    same = jnp.where(row == col, 1.0, 0.0).astype(jnp.bfloat16)
    left = lax.broadcasted_iota(jnp.int32, (size, wide), 1) < dim
    for pair in range(heads // 2):
        columns = slice(pair * wide, (pair + 1) * wide)
        carried = contract(c, high_ref[:, columns]) + contract(c, low_ref[:, columns])
        factor = jnp.where(
            left, factor_ref[:, 2 * pair : 2 * pair + 1], factor_ref[:, 2 * pair + 1 : 2 * pair + 2]
        )
        mixed = pre_ref[:, columns] + carried * factor
        power = contract((mixed * mixed).astype(jnp.bfloat16), same)
        o_ref[:, columns] = (mixed * lax.rsqrt(power * (1.0 / dim) + EPS)).astype(o_ref.dtype)


def small(kernel, name, shapes, scalars, *args, after=()):
    late = list(after)
    return pl.pallas_call(
        kernel,
        in_specs=[SCALARS] * len(scalars) + [ON_CHIP] * len(args) + [HBM] * len(late),
        out_specs=[ON_CHIP] * len(shapes),
        out_shape=[jax.ShapeDtypeStruct(shape, kind) for shape, kind in shapes],
        compiler_params=params(16),
        cost_estimate=pl.CostEstimate(flops=100, bytes_accessed=100, transcendentals=0),
        name=name,
    )(*scalars, *args, *late)


def by_block(n):
    return pl.BlockSpec((Q, n), lambda b: (b, 0))


def once(r, n):
    return pl.BlockSpec((r, n), lambda b: (0, 0))


def recurrence_states(expo, rate, ssd_input, bmat, after):
    heads, length = expo.shape
    width, state = ssd_input.shape[1], bmat.shape[1]
    blocks = length // Q
    return pl.pallas_call(
        states_kernel,
        grid=(blocks,),
        in_specs=[pl.BlockSpec((heads, Q), lambda b: (0, b)), once(1, heads), by_block(width), by_block(state)] + [HBM] * len(after),
        out_specs=[pl.BlockSpec((state, width), lambda b: (jnp.maximum(b - 1, 0), 0)), once(state + 8, width)],
        out_shape=[
            jax.ShapeDtypeStruct(((blocks - 1) * state, width), jnp.float32),
            jax.ShapeDtypeStruct((state + 8, width), jnp.float32),
        ],
        compiler_params=params(60),
        cost_estimate=pl.CostEstimate(
            flops=int(length * 1), bytes_accessed=length, transcendentals=0
        ),
        name="states",
    )(expo, rate[None], ssd_input, bmat, *after)


def recurrence_intra(expo, rate, skip, ssd_input, bmat, cmat, local, after):
    heads, length = expo.shape
    width, state = ssd_input.shape[1], bmat.shape[1]
    blocks = length // Q
    return pl.pallas_call(
        intra_kernel,
        grid=(blocks,),
        in_specs=[
            pl.BlockSpec((heads, Q), lambda b: (0, b)),
            once(1, heads),
            SCALARS,
            once(1, heads),
            by_block(width),
            by_block(state),
            by_block(state),
            pl.BlockSpec((state, width), lambda b: (jnp.maximum(b - 1, 0), 0)),
            HBM,
        ],
        out_specs=[by_block(width), by_block(heads)],
        out_shape=[
            jax.ShapeDtypeStruct((length, width), jnp.float32),
            jax.ShapeDtypeStruct((length, heads), jnp.float32),
        ],
        scratch_shapes=[pltpu.VMEM((1, heads), jnp.float32)],
        compiler_params=params(60),
        cost_estimate=pl.CostEstimate(
            flops=int(length * 1), bytes_accessed=length, transcendentals=0
        ),
        name="intra",
    )(expo, rate[None], rate, skip[None], ssd_input, bmat, cmat, local, after)


def recurrence_final(core, pre, factor, cmat, mine, theirs, other):
    length, width = pre.shape
    heads, state = factor.shape[1], cmat.shape[1]
    return pl.pallas_call(
        final_kernel,
        grid=(length // Q,),
        in_specs=[
            SCALARS,
            by_block(width),
            by_block(heads),
            by_block(state),
            once(*mine.shape),
            once(*theirs.shape),
            once(*other.shape),
        ],
        out_specs=by_block(width),
        out_shape=jax.ShapeDtypeStruct((length, width), jnp.bfloat16),
        scratch_shapes=[pltpu.VMEM((state, width), jnp.bfloat16)] * 2,
        compiler_params=params(24),
        cost_estimate=pl.CostEstimate(
            flops=int(length * 1), bytes_accessed=length, transcendentals=0
        ),
        name="final",
    )(core, pre, factor, cmat, mine, theirs, other)


def on_device(queries, keys, values, ssd_input, bmat, cmat, expo, rate, skip):
    length, width = queries.shape
    devices = lax.axis_size("seq")
    here = lax.axis_index("seq")
    span = W // length
    assert span == 4 and devices % span == 0 and length % (2 * Q) == 0
    assert width == E * (sum(LENT) + sum(RELAYED))
    planes = devices // span
    core, column = here % 2, (here // 2) % 2
    core_1, column_1 = core[None].astype(jnp.int32), column[None].astype(jnp.int32)
    forward = [(i, i + span) for i in range(devices - span)]
    backward = [(j, i) for i, j in forward]
    across = [(i, i ^ 2) for i in range(devices)]
    partner = [(i, i ^ 1) for i in range(devices)]
    send = lambda array, route: lax.ppermute(array, "seq", route)

    starts = [sum(LENT[:i]) for i in range(len(LENT))]
    lent_total, relayed_total = sum(LENT), sum(RELAYED)
    columns = lambda array, s, n: array[:, s * E : (s + n) * E]
    packed = lambda s, n: jnp.concatenate([columns(keys, s, n), columns(values, s, n)], axis=1)

    by_y = [send(packed(s, n), across) for s, n in zip(starts, LENT)]
    asked_first = send(columns(queries, 0, LENT[0]), backward)
    asked_later = send(columns(queries, LENT[0], lent_total - LENT[0]), backward)
    to_z = packed(lent_total, relayed_total)
    by_z = send(to_z, forward)
    partner_k, partner_v = send(keys, partner), send(values, partner)

    side = jnp.stack([core, column]).astype(jnp.int32)
    near = jnp.where(core == 0, 3, 1)
    distance = jnp.stack([jnp.int32(4), near, jnp.int32(2), 4 - near])
    flags = (here >= distance).astype(jnp.int32)

    def lent(i, after, y):
        asked, offset = (asked_first, 0) if i == 0 else (asked_later, starts[i] - LENT[0])
        return lent_heads(
            starts[i], LENT[i], offset, side, queries, asked, keys, values, partner_k, partner_v, y, send(y, partner), after
        )

    expo = expo.T
    local, both = recurrence_states(expo, rate, ssd_input, bmat, [])
    other = send(both, partner)
    partial = [lent(0, local, by_y[0])]
    pre, factor = recurrence_intra(expo, rate, skip, ssd_input, bmat, cmat, local, partial[0][1])
    state = bmat.shape[1]
    wide = ssd_input.shape[1] // 2
    full, brief = jnp.float32, jnp.bfloat16
    chip, rows = small(
        chip_kernel, "chip", [((state + 8, wide), full), ((state + 16, wide), brief)], [core_1], both, other, after=[factor, by_y[1]]
    )
    got = send(rows, across)
    partial.append(lent(1, chip, by_y[1]))
    plane, leaving = small(
        plane_kernel, "plane", [((state + 8, wide), full), ((state, wide), brief)], [column_1], chip, got, after=[partial[1][1]]
    )
    by_a = send(jnp.where(core == 0, to_z, by_z), partner)
    turned = turn(len(RELAYED), column_1, to_z, by_z, factor)
    last_y = [send(part, across) for part in turned]
    last_b = [send(part, partner) for part in last_y]
    entering = jnp.zeros((state, wide), jnp.float32)
    for s in range(planes - 1):
        came = send(leaving, [(s * span + j, (s + 1) * span + j) for j in range(span)])
        if s == 0:
            partial += [lent(i, plane, by_y[i]) for i in range(2, len(LENT))]
        if s < planes - 2:
            entering, leaving = small(
                hop_kernel, "hop", [((state, wide), full), ((state, wide), brief)], [], plane, entering, came
            )
    (entering,) = small(arrive_kernel, "arrive", [((state, wide), full)], [column_1], got, entering, came)
    theirs = send(entering, partner)
    normed_recurrence_output = recurrence_final(core_1, pre, factor, cmat, entering, theirs, other)

    back = [send(message, forward) for _, _, message in partial]
    attn_out = None
    for i, (s, n) in enumerate(zip(starts[:-1], LENT)):
        attn_out = join(s, n, flags, partial[i][0], partial[i][1], back[i], width, partial[-1][1], attn_out)
    for i in range(len(RELAYED)):
        if i == len(RELAYED) - 1:
            attn_out = join(starts[-1], LENT[-1], flags, partial[-1][0], partial[-1][1], back[-1], width, bmat, attn_out)
        offset = sum(RELAYED[:i])
        attn_out = relayed_heads(
            lent_total + offset, offset, relayed_total, flags, queries, keys, values, by_z, by_a, last_y[i], last_b[i], attn_out
        )
    return (attn_out, normed_recurrence_output)


def solution(mesh):
    placed = P(("groups", "seq"), None)
    return jax.shard_map(
        on_device,
        mesh=mesh,
        in_specs=(placed,) * 7 + (P(), P()),
        out_specs=(placed, placed),
        check_vma=False,
    )
```
